32 devices in a mesh: fsdp: 4 (over y, x), seq: 8 (over z, core).
Axes of the slice: x: 2, y: 2, z: 4, core: 2. Of those that a mesh axis runs over, the one named last changes fastest.
Arguments:
- tokens: bfloat16 [8, 1024, 1536], P('fsdp', 'seq'), may hold values from -6 to 6
- gain_one: bfloat16 [1536], P(('fsdp', 'seq')), may hold values from 0.099609375 to 1.8984375
- gain_two: bfloat16 [1536], P(('fsdp', 'seq')), may hold values from 0.099609375 to 1.8984375
- conv_taps: bfloat16 [3, 1536], P(None, ('fsdp', 'seq')), may hold values from -3.5 to 3.5
- w_in: bfloat16 [1536, 4608], P(None, ('fsdp', 'seq')), may hold values from -0.15625 to 0.15625
- w_out: bfloat16 [1536, 1536], P(None, ('fsdp', 'seq')), may hold values from -0.15625 to 0.15625
- w_gate: bfloat16 [1536, 6912], P(None, ('fsdp', 'seq')), may hold values from -0.15625 to 0.15625
- w_up: bfloat16 [1536, 6912], P(None, ('fsdp', 'seq')), may hold values from -0.15625 to 0.15625
- w_down: bfloat16 [6912, 1536], P(None, ('fsdp', 'seq')), may hold values from -0.078125 to 0.078125
- cotangent: bfloat16 [8, 1024, 1536], P('fsdp', 'seq'), may hold values from -6 to 6
Outputs:
- block_out: bfloat16 [8, 1024, 1536], P('fsdp', 'seq')
- grad_tokens: bfloat16 [8, 1024, 1536], P('fsdp', 'seq')
- grad_gain_one: float32 [1536], P(('fsdp', 'seq'))
- grad_gain_two: float32 [1536], P(('fsdp', 'seq'))
- grad_conv: float32 [3, 1536], P(None, ('fsdp', 'seq'))
- grad_w_in: float32 [1536, 4608], P(None, ('fsdp', 'seq'))
- grad_w_out: float32 [1536, 1536], P(None, ('fsdp', 'seq'))
- grad_w_gate: float32 [1536, 6912], P(None, ('fsdp', 'seq'))
- grad_w_up: float32 [1536, 6912], P(None, ('fsdp', 'seq'))
- grad_w_down: float32 [6912, 1536], P(None, ('fsdp', 'seq'))
The draws below stay inside these ranges and needn't reach their ends.
All inputs are finite; a program needn't handle non-finite values.
Results may differ from the reference program's by a relative error of at most 0.0098.
Values may be sent and summed in bfloat16 or wider, within the bound.
No kernel may reach another device: no remote copies, remote signals or barrier semaphores. Data moves between devices by JAX's collectives and lax.ppermute only.
A program may use at most 512 MiB of HBM per device.

```python
import jax
import jax.numpy as jnp
from jax import lax

D = 1536
FF = 6912
LENGTH = 1024
SEQUENCES = 8


def shard_levels(key, extent, pieces, least, high):
    loudness = 1.0
    for dim, shards_of in pieces:
        heights = jax.random.uniform(jax.random.fold_in(jax.random.fold_in(key, 6), dim), (shards_of,), jnp.float32, least / len(pieces), high / len(pieces))
        loudness = loudness * jnp.repeat(jnp.exp(heights), extent[dim] // shards_of).reshape((-1,) + (1,) * (len(extent) - 1 - dim))
    return loudness


def normal_values(rng, extent, spread, limit, cuts=(), held_as=jnp.bfloat16):
    level = shard_levels(rng, extent, cuts, -0.22, 0.18) if cuts else 1.0
    entries = jax.random.normal(rng, extent, jnp.float32) * spread * level
    return jnp.minimum(jnp.maximum(entries, -limit), limit).astype(held_as)


def setup_inputs(seed: int = 0) -> dict:
    keys = jax.random.split(jax.random.key(seed), 11)
    return {
        "tokens": normal_values(keys[0], (SEQUENCES, LENGTH, D), 1.0, 6.0, ((0, 4), (1, 8))),
        "gain_one": jnp.clip(1.0 + 0.18 * jax.random.normal(keys[1], (D,), jnp.float32), 0.099609375, 1.8984375).astype(jnp.bfloat16),
        "gain_two": jnp.clip(1.0 + 0.18 * jax.random.normal(keys[2], (D,), jnp.float32), 0.099609375, 1.8984375).astype(jnp.bfloat16),
        "conv_taps": normal_values(keys[3], (3, D), 3 ** -0.5, 3.5, ((1, 32),)),
        "w_in": normal_values(keys[4], (D, 3 * D), D ** -0.5, 0.15625, ((1, 32),)),
        "w_out": normal_values(keys[5], (D, D), D ** -0.5, 0.15625, ((1, 32),)),
        "w_gate": normal_values(keys[6], (D, FF), D ** -0.5, 0.15625, ((1, 32),)),
        "w_up": normal_values(keys[7], (D, FF), D ** -0.5, 0.15625, ((1, 32),)),
        "w_down": normal_values(keys[8], (FF, D), FF ** -0.5, 0.078125, ((1, 32),)),
        "cotangent": normal_values(keys[9], (SEQUENCES, LENGTH, D), 1.0, 6.0, ((0, 4), (1, 8))),
    }


@jax.custom_vjp
def low(v):
    return lax.optimization_barrier(v.astype(jnp.bfloat16)).astype(jnp.float32)

@jax.custom_vjp
def low_back(v):
    return v

def low_keep(v):
    return (low(v), None)

def low_pass(kept, grad):
    return (grad,)

def back_keep(v):
    return (v, None)

def back_low(kept, grad):
    return (low(grad),)
low.defvjp(low_keep, low_pass)
low_back.defvjp(back_keep, back_low)
epsilon = 1e-05

def matmul(left, right):
    return jnp.dot(left, right, precision=lax.Precision.HIGHEST, preferred_element_type=jnp.float32)

def rms_norm(values, gain):
    scale = lax.rsqrt(lax.optimization_barrier(jnp.mean(values * values, axis=-1, keepdims=True)) + epsilon)
    return values * scale * gain

def forward(hidden_in, gain_one, gain_two, conv_taps, w_in, w_out, w_gate, w_up, w_down):
    width = hidden_in.shape[-1]
    normed_a = low(rms_norm(hidden_in, gain_one))
    mixed = low_back(matmul(normed_a, w_in))
    b_part = mixed[:, :width]
    c_part = mixed[:, width:2 * width]
    x_part = mixed[:, 2 * width:]
    gated = low(b_part * x_part)
    padded = jnp.pad(gated, ((2, 0), (0, 0)))
    conv = conv_taps[0] * padded[:-2] + conv_taps[1] * padded[1:-1] + conv_taps[2] * padded[2:]
    branch_y = low(c_part * conv)
    branch_o = low_back(matmul(branch_y, w_out))
    second = hidden_in + branch_o
    normed_u = low(rms_norm(second, gain_two))
    gate_val = low_back(matmul(normed_u, w_gate))
    up_val = low_back(matmul(normed_u, w_up))
    hidden = low(jax.nn.silu(gate_val) * up_val)
    return second + matmul(hidden, w_down)

def reference(tokens, gain_one, gain_two, conv_taps, w_in, w_out, w_gate, w_up, w_down, cotangent):
    params = tuple((p.astype(jnp.float32) for p in (gain_one, gain_two, conv_taps, w_in, w_out, w_gate, w_up, w_down)))

    def one_seq(carry, pair):
        sequence, seq_cot = pair
        result, pull = jax.vjp(forward, sequence.astype(jnp.float32), *params)
        grads = pull(seq_cot.astype(jnp.float32))
        carry = tuple((c + g for c, g in zip(carry, grads[1:])))
        return (carry, (result.astype(jnp.bfloat16), grads[0].astype(jnp.bfloat16)))
    start = tuple((jnp.zeros_like(p) for p in params))
    totals, (outputs, input_grads) = lax.scan(one_seq, start, (tokens, cotangent))
    return (outputs, input_grads, totals[0], totals[1], totals[2], totals[3], totals[4], totals[5], totals[6], totals[7])
```

```python
import jax
import jax.numpy as jnp
from jax import lax
from jax.sharding import Mesh, PartitionSpec as P

epsilon = 1e-05
every = ("fsdp", "line", "core")
bf16 = jnp.bfloat16
f32 = jnp.float32


def product(left, right):
    return jnp.dot(left, right, preferred_element_type=f32)


def right_trans(left, right):
    return lax.dot_general(left, right, (((1,), (1,)), ((), ())), preferred_element_type=f32)


def left_trans(left, right):
    return lax.dot_general(left, right, (((0,), (0,)), ((), ())), preferred_element_type=f32)


def cuts(rows, parts):
    ends = [min(rows, -(-rows * (p + 1) // (16 * parts)) * 16) for p in range(parts)]
    return list(zip([0] + ends[:-1], ends))


def flip(block, axis, bit):
    size = lax.axis_size(axis)
    return lax.ppermute(block, axis, [(i, i ^ bit) for i in range(size)])


def cube_gather(block, axis):
    size = lax.axis_size(axis)
    bits = size.bit_length() - 1
    held = [{0: block[a:b]} for a, b in cuts(block.shape[0], bits)]
    for step in range(bits):
        for p in range(bits):
            bit = 1 << (p + step) % bits
            slots = sorted(held[p])
            other = flip(jnp.stack([held[p][r] for r in slots]), axis, bit)
            held[p].update({r ^ bit: other[n] for n, r in enumerate(slots)})
    return jnp.stack([jnp.concatenate([h[r] for h in held], 0) for r in range(size)])


def cube_scatter(slots, axis):
    size = lax.axis_size(axis)
    bits = size.bit_length() - 1
    held = [{r: slots[r, a:b] for r in range(size)} for a, b in cuts(slots.shape[1], bits)]
    for step in reversed(range(bits)):
        for p in range(bits):
            bit = 1 << (p + step) % bits
            keep = sorted(r for r in held[p] if not r & bit)
            other = flip(jnp.stack([held[p][r | bit].astype(bf16) for r in keep]), axis, bit)
            held[p] = {r: held[p][r] + other[n].astype(f32) for n, r in enumerate(keep)}
    return jnp.concatenate([h[0] for h in held], 0)


def line_gather(block, axis):
    size = lax.axis_size(axis)
    me = lax.axis_index(axis)
    up = [(i, i + 1) for i in range(size - 1)]
    down = [(i + 1, i) for i in range(size - 1)]
    left, right = [block], [block]
    for s in range(1, size):
        left.append(lax.ppermute(left[-1], axis, up[s - 1 :]))
        right.append(lax.ppermute(right[-1], axis, down[: size - s]))
    return jnp.stack([block] + [jnp.where(me >= s, left[s], right[size - s]) for s in range(1, size)])


def line_scatter(slots, axis):
    size = lax.axis_size(axis)
    up = [(i, i + 1) for i in range(size - 1)]
    down = [(i + 1, i) for i in range(size - 1)]
    left = right = None
    for t in range(1, size):
        to_left = slots[size - t] if left is None else slots[size - t] + left.astype(f32)
        to_right = slots[t] if right is None else slots[t] + right.astype(f32)
        left = lax.ppermute(to_left.astype(bf16), axis, down[size - 1 - t :])
        right = lax.ppermute(to_right.astype(bf16), axis, up[:t])
    return slots[0] + left.astype(f32) + right.astype(f32)


def exchange(blocks, axis):
    size = lax.axis_size(axis)
    me = lax.axis_index(axis)
    own = lax.dynamic_index_in_dim(blocks, me, 0, keepdims=False)
    got = jnp.zeros_like(blocks)
    got = lax.dynamic_update_index_in_dim(got, own, me, 0)
    for k in range(1, size):
        sent = lax.dynamic_index_in_dim(blocks, (me + k) % size, 0, keepdims=False)
        came = lax.ppermute(sent, axis, [(i, (i + k) % size) for i in range(size)])
        got = lax.dynamic_update_index_in_dim(got, came, (me - k) % size, 0)
    return got


def on_device(tokens, gain_one, gain_two, conv_taps, w_in, w_out, w_gate, w_up, w_down, cotangent):
    seqs, group, width = tokens.shape
    rows = seqs * group
    lanes, line = lax.axis_size("fsdp"), lax.axis_size("line")
    pieces = 2 * line
    count = lanes * pieces
    feats = width // count
    mine = width // lanes
    hid = w_gate.shape[1]
    wide = lanes * 2 * hid
    f_index = lax.axis_index("fsdp")
    index = lax.axis_index(every)

    in_blocks = w_in.T.reshape(3, feats, width)
    routes = [[(k, (3 * k + j) % count) for k in range(count)] for j in range(3)]
    came = jnp.stack([lax.ppermute(in_blocks[j], every, routes[j]) for j in range(3)])
    in_parts = [
        lax.dynamic_index_in_dim(came, (index + p * count) % 3, 0, keepdims=False) for p in range(3)
    ]
    smalls = jnp.concatenate([gain_one[None], gain_two[None], conv_taps], 0)
    smalls = jnp.pad(smalls, ((0, 11), (0, mine - feats)))
    out_blocks = w_out.T.reshape(feats, lanes, mine).transpose(1, 0, 2)
    out_blocks = jnp.concatenate([out_blocks, jnp.broadcast_to(smalls, (lanes, 16, mine))], 1)
    out_blocks = exchange(out_blocks, "fsdp").transpose(1, 0, 2).reshape(feats + 16, width)
    mixer_w = lax.all_gather(
        jnp.concatenate(in_parts + [out_blocks], 0), ("line", "core"), axis=0
    )
    full_in = mixer_w[:, : 3 * feats].reshape(pieces, 3, feats, width)
    full_in = full_in.transpose(1, 0, 2, 3).reshape(3, mine, width)
    full_out = mixer_w[:, 3 * feats : 4 * feats].reshape(pieces, feats, lanes, mine)
    full_out = full_out.transpose(2, 0, 1, 3).reshape(width, mine)
    small = mixer_w[:, 4 * feats : 4 * feats + 5].reshape(pieces, 5, lanes, mine)[..., :feats]
    small = small.transpose(1, 2, 0, 3).reshape(5, width).astype(f32)
    taps = lax.dynamic_slice_in_dim(small[2:], f_index * mine, mine, 1)

    down_blocks = w_down.reshape(lanes, line, 2 * hid, feats).transpose(1, 3, 0, 2)
    down_blocks = exchange(down_blocks.reshape(line, feats, wide), "line")
    full_down = lax.all_gather(down_blocks, ("fsdp", "core"), axis=0)
    full_down = full_down.reshape(lanes, 2, line, feats, wide).transpose(0, 2, 1, 3, 4)
    full_down = full_down.reshape(width, wide)
    gate_up = lax.all_gather(
        jnp.concatenate([w_gate.T, w_up.T], 0), ("fsdp", "core"), axis=0
    )
    full_gate = gate_up[:, :hid].reshape(wide, width)
    full_up = gate_up[:, hid:].reshape(wide, width)

    token_rows = tokens.reshape(rows, width)
    all_tokens = cube_gather(token_rows, "fsdp").reshape(lanes * rows, width)
    all_in = all_tokens.astype(f32)
    scale_all = lax.rsqrt(jnp.mean(all_in * all_in, axis=-1, keepdims=True) + epsilon)
    unit_all = all_in * scale_all
    normed_a = (unit_all * small[0]).astype(bf16)
    b_part = right_trans(normed_a, full_in[0])
    c_part = right_trans(normed_a, full_in[1])
    x_part = right_trans(normed_a, full_in[2])
    every_seq = lanes * seqs
    gated = (b_part * x_part).astype(bf16).reshape(every_seq, group, mine)
    onward = [(i, i + 1) for i in range(pieces - 1)]
    back = [(i + 1, i) for i in range(pieces - 1)]
    before = lax.ppermute(gated[:, group - 2 :, :], ("line", "core"), onward)
    extended = jnp.concatenate([before, gated], 1).astype(f32)
    conv = (
        taps[0] * extended[:, :group]
        + taps[1] * extended[:, 1 : group + 1]
        + taps[2] * extended[:, 2:]
    ).reshape(lanes * rows, mine)
    branch_y = (c_part * conv).astype(bf16)
    branch_o = cube_scatter(
        right_trans(branch_y, full_out).reshape(lanes, rows, width), "fsdp"
    )
    hidden_in = token_rows.astype(f32)
    second = hidden_in + branch_o
    scale_two = lax.rsqrt(jnp.mean(second * second, axis=-1, keepdims=True) + epsilon)
    unit_two = second * scale_two
    normed_u = (unit_two * small[1]).astype(bf16)

    cot_rows = cotangent.reshape(rows, width)
    all_cot = line_gather(cot_rows, "line").reshape(line * rows, width)
    dhidden = product(all_cot, full_down)
    all_u = line_gather(normed_u, "line").reshape(line * rows, width)
    gate_val = right_trans(all_u, full_gate)
    up_val = right_trans(all_u, full_up)
    sigmoid_g = jax.nn.sigmoid(gate_val)
    silu_g = gate_val * sigmoid_g
    hidden = (silu_g * up_val).astype(bf16)
    dgate = (dhidden * up_val * sigmoid_g * (1.0 + gate_val * (1.0 - sigmoid_g))).astype(bf16)
    dup_val = (dhidden * silu_g).astype(bf16)
    dunit = product(dgate, full_gate) + product(dup_val, full_up)
    dunit = line_scatter(dunit.reshape(line, rows, width), "line")
    part_out = right_trans(hidden, full_down)
    part_out = line_scatter(part_out.reshape(line, rows, width), "line")
    block_out = (second + part_out).astype(bf16).reshape(seqs, group, width)

    g_down = left_trans(all_cot, hidden).astype(bf16)
    g_down = g_down.reshape(lanes, line, 2, feats, wide).transpose(0, 2, 1, 3, 4)
    g_down = lax.psum_scatter(
        g_down.reshape(lanes * 2, line, feats, wide), ("fsdp", "core"), scatter_dimension=0
    )
    g_down = exchange(g_down, "line").reshape(line, feats, lanes, 2 * hid)
    grad_down = g_down.transpose(2, 0, 3, 1).reshape(count * hid, feats).astype(f32)
    g_gate = left_trans(dgate, all_u).astype(bf16).reshape(lanes * 2, hid, width)
    g_up = left_trans(dup_val, all_u).astype(bf16).reshape(lanes * 2, hid, width)
    g_gu = lax.psum_scatter(
        jnp.concatenate([g_gate, g_up], 1), ("fsdp", "core"), scatter_dimension=0
    )
    grad_gate = g_gu[:hid].T.astype(f32)
    grad_up = g_gu[hid:].T.astype(f32)

    grad_two = jnp.sum(dunit * unit_two, axis=0)
    dnorm_two = dunit * small[1]
    dsecond = cot_rows.astype(f32) + scale_two * (
        dnorm_two - unit_two * jnp.mean(dnorm_two * unit_two, axis=-1, keepdims=True)
    )
    all_branch = cube_gather(dsecond.astype(bf16), "fsdp").reshape(lanes * rows, width)
    dy_rows = product(all_branch, full_out)
    dconv = (dy_rows * c_part).reshape(every_seq, group, mine)
    dc_part = dy_rows * conv
    after = lax.ppermute(dconv[:, :2, :], ("line", "core"), back)
    dext = jnp.concatenate([dconv, after], 1)
    dgated = (
        taps[2] * dext[:, :group] + taps[1] * dext[:, 1 : group + 1] + taps[0] * dext[:, 2:]
    ).reshape(lanes * rows, mine)
    grad_taps = jnp.stack(
        [jnp.sum(dconv * extended[:, k : k + group], axis=(0, 1)) for k in range(3)], 0
    )
    dmixed = [(dgated * x_part).astype(bf16), dc_part.astype(bf16), (dgated * b_part).astype(bf16)]
    dnormed = sum(product(dmixed[p], full_in[p]) for p in range(3))
    grad_one = jnp.sum(dnormed * unit_all, axis=0)
    dnormed = cube_scatter(dnormed.reshape(lanes, rows, width), "fsdp")
    scale_one = lax.rsqrt(jnp.mean(hidden_in * hidden_in, axis=-1, keepdims=True) + epsilon)
    unit_one = hidden_in * scale_one
    dnorm_one = dnormed * small[0]
    dinput = dsecond + scale_one * (
        dnorm_one - unit_one * jnp.mean(dnorm_one * unit_one, axis=-1, keepdims=True)
    )
    grad_tokens = dinput.astype(bf16).reshape(seqs, group, width)

    g_in = jnp.stack([left_trans(d, normed_a).astype(bf16) for d in dmixed])
    g_in = g_in.reshape(3, pieces, feats, width).transpose(1, 0, 2, 3)
    g_out = left_trans(all_branch, branch_y).astype(bf16).reshape(lanes, pieces, feats, mine)
    g_out = g_out.transpose(1, 2, 0, 3).reshape(pieces, feats, width)
    gains = jnp.stack([grad_one, grad_two]).reshape(2, lanes, pieces, feats)
    gains = gains.transpose(2, 1, 0, 3).reshape(pieces, lanes * 2 * feats)
    g_taps = grad_taps.reshape(3, pieces, feats).transpose(1, 0, 2).reshape(pieces, 3 * feats)
    g_small = jnp.concatenate([gains, g_taps], 1)
    g_small = jnp.pad(g_small[:, None], ((0, 0), (0, 15), (0, width - g_small.shape[1])))
    g_mixer = lax.psum_scatter(
        jnp.concatenate(
            [g_in.reshape(pieces, 3 * feats, width), g_out, g_small.astype(bf16)], 1
        ),
        ("line", "core"),
        scatter_dimension=0,
    )
    g_in = g_mixer[: 3 * feats].reshape(3, feats, width)
    homes = [[(d, k) for k, d in route] for route in routes]
    parts = []
    for j in range(3):
        p = ((j - index) * pow(count, -1, 3)) % 3
        block = lax.dynamic_index_in_dim(g_in, p, 0, keepdims=False)
        parts.append(lax.ppermute(block, every, homes[j]))
    grad_in = jnp.concatenate(parts, 0).T.astype(f32)
    g_out = g_mixer[3 * feats : 4 * feats].reshape(feats, lanes, mine).transpose(1, 0, 2)
    g_small = g_mixer[4 * feats]
    gains = g_small[: lanes * 2 * feats].reshape(lanes, 1, 2 * feats)
    gains = jnp.pad(gains, ((0, 0), (0, 15), (0, mine - 2 * feats)))
    got = exchange(jnp.concatenate([g_out, gains], 1), "fsdp")
    grad_out = got[:, :feats].transpose(0, 2, 1).reshape(width, feats).astype(f32)
    gains = jnp.sum(got[:, feats].astype(f32), axis=0)
    grad_taps = g_small[lanes * 2 * feats :][: 3 * feats].reshape(3, feats).astype(f32)
    return (
        block_out,
        grad_tokens,
        gains[:feats],
        gains[feats : 2 * feats],
        grad_taps,
        grad_in,
        grad_out,
        grad_gate,
        grad_up,
        grad_down,
    )


def solution(mesh):
    lanes, pieces = mesh.devices.shape
    fine = Mesh(mesh.devices.reshape(lanes, pieces // 2, 2), every)
    token = P("fsdp", ("line", "core"), None)
    vector = P(every)
    columns = P(None, every)
    return jax.shard_map(
        on_device,
        mesh=fine,
        in_specs=(token, vector, vector) + (columns,) * 6 + (token,),
        out_specs=(token, token, vector, vector) + (columns,) * 6,
        check_vma=False,
    )
```

```python
import functools

import jax
import jax.numpy as jnp
from jax import lax
from jax.experimental import pallas as pl
from jax.experimental.pallas import tpu as pltpu
from jax.sharding import Mesh, PartitionSpec as P

epsilon = 1e-05
every = ("fsdp", "line", "core")
bf16 = jnp.bfloat16
f32 = jnp.float32
vmem_bytes = 58 * 2**20


def dot(left, right):
    return jnp.dot(left, right, preferred_element_type=f32)


def dot_nt(left, right):
    return lax.dot_general(left, right, (((1,), (1,)), ((), ())), preferred_element_type=f32)


def dot_tn(left, right):
    return lax.dot_general(left, right, (((0,), (0,)), ((), ())), preferred_element_type=f32)


def tie(block, *earlier):
    anywhere = pl.BlockSpec(memory_space=pl.ANY)
    return pl.pallas_call(
        lambda *refs: None,
        in_specs=[anywhere] * (1 + len(earlier)),
        out_specs=anywhere,
        out_shape=jax.ShapeDtypeStruct(block.shape, block.dtype),
        input_output_aliases={0: 0},
    )(block, *earlier)


def flip(block, axis, bits):
    size = lax.axis_size(axis)
    return lax.ppermute(block, axis, [(i, i ^ bits) for i in range(size)])


def gather(block, axis):
    return [block] + [flip(block, axis, r) for r in range(1, lax.axis_size(axis))]


def scatter(slots, axis):
    return [slots[0]] + [flip(slots[r], axis, r) for r in range(1, lax.axis_size(axis))]


def total(terms):
    return sum(t.astype(f32) for t in terms)


def exchange(blocks, axis):
    size = lax.axis_size(axis)
    me = lax.axis_index(axis)
    came = []
    for r in range(size):
        sent = lax.dynamic_index_in_dim(blocks, me ^ r, 0, keepdims=False)
        came.append(flip(sent, axis, r) if r else sent)
    out = []
    for d in range(size):
        block = came[0]
        for r in range(1, size):
            block = jnp.where(me ^ r == d, came[r], block)
        out.append(block)
    return out


def whole(shape):
    return pl.BlockSpec(shape, lambda *_: (0,) * len(shape))


def kernel_call(body, grid, ins, outs, scratch, flops, *args):
    shapes = [jax.ShapeDtypeStruct(shape, dtype) for shape, dtype, _ in outs]
    moved = sum(a.size * a.dtype.itemsize for a in args)
    moved += sum(s.size * s.dtype.itemsize for s in shapes)
    return pl.pallas_call(
        body,
        grid=grid,
        in_specs=ins,
        out_specs=[spec for _, _, spec in outs],
        out_shape=shapes,
        scratch_shapes=scratch,
        compiler_params=pltpu.CompilerParams(
            dimension_semantics=("arbitrary",) * len(grid), vmem_limit_bytes=vmem_bytes
        ),
        cost_estimate=pl.CostEstimate(flops=flops, bytes_accessed=moved, transcendentals=0),
    )(*args)


def shifted(block, distance, edge):
    rows = block.shape[0]
    moved = pltpu.roll(block, distance % rows, 0)
    row = lax.broadcasted_iota(jnp.int32, block.shape, 0)
    for n in range(abs(distance)):
        at = n if distance > 0 else rows - abs(distance) + n
        moved = jnp.where(row == at, edge[n : n + 1], moved)
    return moved


def mixer_forward(seqs, group, lanes, line, in_place, *refs):
    tok_refs, (gain_ref, taps_ref), refs = refs[:lanes], refs[lanes : lanes + 2], refs[lanes + 2 :]
    if in_place:
        places_ref, source_refs, refs = refs[0], refs[1 : 1 + 2 * line], refs[1 + 2 * line :]
        win_ref, wout_ref = refs[lanes + 8 : lanes + 10]
        bring_weights(2 * line, places_ref, source_refs, win_ref, wout_ref, refs[-1])
    else:
        (win_ref, wout_ref), refs = refs[:2], refs[2:]
    part_refs, refs = refs[:lanes], refs[lanes:]
    norm_ref, b_ref, c_ref, x_ref, conv_ref, gated_ref, halo_ref, y_ref = refs[:8]
    tok_ref = refs[10 if in_place else 8]
    pick(tok_refs, tok_ref)
    rows = seqs * group
    h = tok_ref[...].astype(f32)
    unit = h * lax.rsqrt(jnp.mean(h * h, axis=-1, keepdims=True) + epsilon)
    norm = (unit * gain_ref[...]).astype(bf16)
    norm_ref[0] = norm[:rows]
    b_all, x_all = dot_nt(norm, win_ref[0]), dot_nt(norm, win_ref[2])
    c_part = dot_nt(norm[:rows], win_ref[1])
    b_ref[0], c_ref[0], x_ref[0] = b_all[:rows], c_part, x_all[:rows]
    gated = (b_all * x_all).astype(bf16)
    gated_ref[0], halo_ref[0] = gated[:rows], gated[rows:]
    halo = gated[rows:].astype(f32)
    for q in range(seqs):
        at = slice(q * group, (q + 1) * group)
        now = gated[at].astype(f32)
        edge = halo[2 * q : 2 * q + 2]
        conv = (
            taps_ref[0:1] * shifted(now, 2, edge)
            + taps_ref[1:2] * shifted(now, 1, edge[1:])
            + taps_ref[2:3] * now
        )
        conv_ref[0, at] = conv
        y_ref[0, at] = (c_part[at] * conv).astype(bf16)
    hand(dot_nt(y_ref[0], wout_ref[...]).astype(bf16), part_refs)


def merged(ref):
    n, units, width = ref.shape
    return ref[...].reshape(n * units, width)


def hidden_gradient(line, *refs):
    cot_refs, down_ref, out_refs = refs[:line], refs[line], refs[line + 1 :]
    w_down = merged(down_ref)
    rows = cot_refs[0].shape[0]
    for r in range(line):
        at = slice(r // 2 * rows, (r // 2 + 1) * rows)
        out_refs[r % 2][0, at] = dot_nt(cot_refs[r][...], w_down)


def add_up(acc_ref, at, part, out_ref):
    j = pl.program_id(0)

    @pl.when(j == 0)
    def _():
        acc_ref[at] = part

    @pl.when(j == 1)
    def _():
        out_ref[...] = (acc_ref[at] + part).astype(bf16)


def feed_forward(n, *refs):
    u_refs, (gate_ref, up_ref, dh_ref), refs = refs[:n], refs[n : n + 3], refs[n + 3 :]
    (hid_ref, dg_ref, dup_ref), du_refs, acc_ref = refs[:3], refs[3 : 3 + n], refs[3 + n]
    w_gate, w_up = merged(gate_ref), merged(up_ref)
    rows = u_refs[0].shape[0]
    for r in range(n):
        at = slice(r * rows, (r + 1) * rows)
        gate = dot_nt(u_refs[r][...], w_gate)
        up = dot_nt(u_refs[r][...], w_up)
        dh = dh_ref[0, at]
        sig = jax.nn.sigmoid(gate)
        silu = gate * sig
        hid_ref[0, at] = (silu * up).astype(bf16)
        dgate = (dh * up * sig * (1.0 + gate * (1.0 - sig))).astype(bf16)
        dup = (dh * silu).astype(bf16)
        dg_ref[0, at] = dgate
        dup_ref[0, at] = dup
        add_up(acc_ref, at, dot(dgate, w_gate) + dot(dup, w_up), du_refs[r])


def feed_forward_out(line, *refs):
    hid_refs, down_ref, out_refs, acc_ref = refs[:2], refs[2], refs[3 : 3 + line], refs[3 + line]
    w_down = merged(down_ref)
    rows = out_refs[0].shape[0]
    for r in range(line):
        part = dot(hid_refs[r % 2][0, r // 2 * rows : (r // 2 + 1) * rows], w_down)
        add_up(acc_ref, slice(r * rows, (r + 1) * rows), part, out_refs[r])


def feed_forward_grads(line, *refs):
    u_refs, cot_refs, refs = refs[:line], refs[line : 2 * line], refs[2 * line :]
    halves, out_ref, (u_all, cot_all) = (refs[:3], refs[3:6]), refs[6], refs[7:]
    rows = u_refs[0].shape[0]

    @pl.when(pl.program_id(0) == 0)
    def _():
        for r in range(line):
            at = slice(r // 2 * rows, (r // 2 + 1) * rows)
            u_all[r % 2, at] = u_refs[r][...]
            cot_all[r % 2, at] = cot_refs[r][...]

    n, units, width = out_ref.shape
    units //= 3
    for k, right in enumerate((cot_all, u_all, u_all)):
        part = sum(dot_tn(halves[h][k][0], right[h]) for h in range(2))
        at = (k - 1) % 3 * units
        out_ref[:, at : at + units] = part.astype(bf16).reshape(n, units, width)


def pick(slot_refs, out_ref):
    for r, ref in enumerate(slot_refs):

        @pl.when(pl.program_id(0) == r)
        def _(ref=ref):
            out_ref[...] = ref[...]


def hand(block, out_refs):
    for r, ref in enumerate(out_refs):

        @pl.when(pl.program_id(0) == r)
        def _(ref=ref):
            ref[...] = block


def bring_weights(pieces, places_ref, sources, win_ref, wout_ref, sems):
    width, mine = wout_ref.shape
    feats = mine // pieces
    copies = []
    for k, source in enumerate(sources):
        s = places_ref[k]
        for p in range(3):
            rows = pl.ds(pl.multiple_of(s * feats, 16), feats)
            copies.append((source.at[pl.ds(p * feats, feats)], win_ref.at[p, rows]))
        for f in range(width // mine):
            rows = pl.ds(pl.multiple_of((f * pieces + s) * feats, 16), feats)
            columns = source.at[pl.ds(3 * feats, feats), pl.ds(f * mine, mine)]
            copies.append((columns, wout_ref.at[rows]))
    copies = [pltpu.make_async_copy(a, b, sems.at[n]) for n, (a, b) in enumerate(copies)]

    @pl.when(pl.program_id(0) == 0)
    def _():
        for copy in copies:
            copy.start()
        for copy in copies:
            copy.wait()


def mixer_backward_one(lanes, *refs):
    branch_refs, (wout_ref, c_ref, conv_ref, dconv_ref, dc_ref, now_ref) = refs[:lanes], refs[lanes:]
    pick(branch_refs, now_ref)
    dy = dot(now_ref[...], wout_ref[...])
    dconv_ref[0] = dy * c_ref[0]
    dc_ref[0] = (dy * conv_ref[0]).astype(bf16)


def mixer_backward_two(seqs, group, pieces, lanes, *refs):
    tok_refs, branch_refs, refs = refs[:lanes], refs[lanes : 2 * lanes], refs[2 * lanes :]
    (dconv_ref, ahead_ref, dc_ref, b_ref, x_ref, gated_ref, halo_ref, taps_ref, two_ref) = refs[:9]
    (win_ref, norm_ref, y_ref), refs = refs[9:12], refs[12:]
    part_refs, (out_ref, dm_ref, one_ref, dt_ref, tok_ref) = refs[:lanes], refs[lanes:]
    pick(tok_refs, tok_ref)
    r = pl.program_id(0)
    rows = seqs * group
    width = norm_ref.shape[2]
    mine = win_ref.shape[1]

    @pl.when(r == 0)
    def _():
        one_ref[...] = jnp.zeros_like(one_ref)
        dt_ref[...] = jnp.zeros_like(dt_ref)

    for q in range(seqs):
        at = slice(q * group, (q + 1) * group)
        now = dconv_ref[0, at]
        edge = ahead_ref[0, 2 * q : 2 * q + 2]
        dgated = (
            taps_ref[2:3] * now
            + taps_ref[1:2] * shifted(now, -1, edge)
            + taps_ref[0:1] * shifted(now, -2, edge)
        )
        dm_ref[0, r, at] = (dgated * x_ref[0, at]).astype(bf16)
        dm_ref[2, r, at] = (dgated * b_ref[0, at]).astype(bf16)
        held = gated_ref[0, at].astype(f32)
        past = halo_ref[0].astype(f32)[2 * q : 2 * q + 2]
        for k, block in enumerate((shifted(held, 2, past), shifted(held, 1, past[1:]), held)):
            dt_ref[k : k + 1] += jnp.sum(now * block, axis=0, keepdims=True)
    dm_ref[1, r] = dc_ref[0]
    da = sum(dot(dm_ref[p, r], win_ref[p]) for p in range(3))
    hand(da.astype(bf16), part_refs)
    h = tok_ref[:rows].astype(f32)
    unit = h * lax.rsqrt(jnp.mean(h * h, axis=-1, keepdims=True) + epsilon)
    one_ref[...] += jnp.sum(da * unit, axis=0, keepdims=True)

    @pl.when(r == pl.num_programs(0) - 1)
    def _():
        slots = norm_ref.shape[0]
        feats = mine // pieces
        norm = norm_ref[...].reshape(slots * rows, width)
        for p in range(3):
            g_in = dot_tn(dm_ref[p].reshape(slots * rows, mine), norm).astype(bf16)
            for s in range(pieces):
                out_ref[s, p * feats : (p + 1) * feats] = g_in[s * feats : (s + 1) * feats]
        g_out = sum(dot_tn(branch_refs[f][...], y_ref[f]) for f in range(lanes)).astype(bf16)
        small = jnp.concatenate([one_ref[...], two_ref[...], jnp.zeros((14, width), f32)], 0)
        small = small.astype(bf16)
        for s in range(pieces):
            for f in range(lanes):
                a = (f * pieces + s) * feats
                out_ref[s, 3 * feats : 4 * feats, f * mine : (f + 1) * mine] = g_out[a : a + feats]
            out_ref[s, 4 * feats :] = small
            out_ref[s, 4 * feats + 2 : 4 * feats + 5, :mine] = dt_ref[...].astype(bf16)


def on_device(tokens, gain_one, gain_two, conv_taps, w_in, w_out, w_gate, w_up, w_down, cotangent):
    seqs, group, width = tokens.shape
    rows = seqs * group
    lanes, line = lax.axis_size("fsdp"), lax.axis_size("line")
    pieces = 2 * line
    count = lanes * pieces
    feats = width // count
    mine = width // lanes
    hid = w_gate.shape[1]
    units = -(-hid // 16) * 16
    blocks = lanes * 2
    f_index = lax.axis_index("fsdp")
    s_index = lax.axis_index(("line", "core"))
    index = lax.axis_index(every)
    onward = [(i, i + 1) for i in range(pieces - 1)]
    back = [(i + 1, i) for i in range(pieces - 1)]

    in_blocks = w_in.T.reshape(3, feats, width)
    routes = [[(k, (3 * k + j) % count) for k in range(count)] for j in range(3)]
    came = jnp.stack([lax.ppermute(in_blocks[j], every, routes[j]) for j in range(3)])
    in_parts = [
        lax.dynamic_index_in_dim(came, (index + p * count) % 3, 0, keepdims=False) for p in range(3)
    ]
    smalls = jnp.concatenate([gain_one[None], gain_two[None], conv_taps], 0)
    smalls = jnp.pad(smalls, ((0, 11), (0, mine - feats)))
    out_blocks = w_out.T.reshape(feats, lanes, mine).transpose(1, 0, 2)
    out_blocks = jnp.concatenate([out_blocks, jnp.broadcast_to(smalls, (lanes, 16, mine))], 1)
    out_blocks = jnp.concatenate(exchange(out_blocks, "fsdp"), 1)
    edge = lax.ppermute(tokens[:, group - 2 :], ("line", "core"), onward).reshape(2 * seqs, width)
    edge = jnp.pad(edge, ((0, -2 * seqs % 16), (0, 0)))
    mixer_own = tie(jnp.concatenate(in_parts + [out_blocks], 0), edge)
    down_rows = tie(w_down.T.reshape(feats, count, hid).transpose(1, 0, 2), mixer_own)
    down_rows = lax.all_to_all(down_rows, every, 0, 0, tiled=True)
    mixer_slots = gather(mixer_own, "line")

    token_rows = tokens.reshape(rows, width)
    token_slots = gather(tie(jnp.concatenate([token_rows, edge], 0), mixer_own), "fsdp")

    swapped = list(flip(jnp.stack(mixer_slots[:1] + mixer_slots[1::2]), "core", 1))
    late = flip(tie(jnp.stack(mixer_slots[2::2]), *token_slots[1:], down_rows), "core", 1)
    swapped = [swapped[0]] + [s for pair in zip(swapped[1:], list(late) + [None]) for s in pair][:-1]
    cot_rows = cotangent.reshape(rows, width)
    cot_slots = gather(tie(cot_rows, *mixer_slots[1:]), "line")
    z_index, c_index = lax.axis_index("line"), lax.axis_index("core")
    near = jnp.arange(line, dtype=jnp.int32) ^ z_index
    places = jnp.concatenate([2 * near + c_index, 2 * near + 1 - c_index])
    small = jnp.stack([m[4 * feats : 4 * feats + 5] for m in mixer_slots + swapped])
    small = small.reshape(pieces, 5, lanes, mine)[..., :feats].reshape(pieces, 5 * lanes * feats)
    order = (places[None] == jnp.arange(pieces)[:, None]).astype(bf16)
    small = dot(order, small).reshape(pieces, 5, lanes, feats)
    small = small.transpose(1, 2, 0, 3).reshape(5, width)
    taps = lax.dynamic_slice_in_dim(small[2:], f_index * mine, mine, 1)
    anywhere = pl.BlockSpec(memory_space=pl.ANY)
    in_place = feats % 16 == 0 and mine % 128 == 0
    if in_place:
        weights = [places] + mixer_slots + swapped
        weight_specs = [pl.BlockSpec(memory_space=pltpu.SMEM)] + [anywhere] * pieces
        weight_outs = [((3, mine, width), bf16, whole((3, mine, width)))]
        weight_outs += [((width, mine), bf16, whole((width, mine)))]
        weight_scratch = [pltpu.SemaphoreType.DMA((pieces * (3 + lanes),))]
    else:
        mixer_w = jnp.stack(mixer_slots + swapped)[jnp.argsort(places)]
        full_in = mixer_w[:, : 3 * feats].reshape(pieces, 3, feats, width)
        full_in = full_in.transpose(1, 0, 2, 3).reshape(3, mine, width)
        full_out = mixer_w[:, 3 * feats : 4 * feats].reshape(pieces, feats, lanes, mine)
        full_out = full_out.transpose(2, 0, 1, 3).reshape(width, mine)
        weights = [full_in, full_out]
        weight_specs = [whole((3, mine, width)), whole((width, mine))]
        weight_outs = weight_scratch = []

    pad = ((0, units - hid), (0, 0))
    gate_up = jnp.concatenate([jnp.pad(w, pad) for w in (w_gate.T, w_up.T)], 0)
    gate_up = lax.all_gather(gate_up, ("fsdp", "core"), axis=0)

    more = token_slots[0].shape[0]
    everyone = lanes * rows
    slot = lambda *shape: pl.BlockSpec((1,) + shape, lambda r: (r,) + (0,) * len(shape))
    per_slot = lambda dtype, *shape: ((lanes,) + shape, dtype, slot(*shape))
    flat = lambda n, count: [((n, width), bf16, whole((n, width)))] * count
    made = kernel_call(
        functools.partial(mixer_forward, seqs, group, lanes, line, in_place),
        (lanes,),
        [whole((more, width))] * lanes + [whole((1, width)), whole((3, mine))] + weight_specs,
        flat(rows, lanes)
        + [per_slot(bf16, rows, width)]
        + [per_slot(f32, rows, mine)] * 4
        + [per_slot(bf16, rows, mine), per_slot(bf16, more - rows, mine), per_slot(bf16, rows, mine)]
        + weight_outs,
        [pltpu.VMEM((more, width), bf16)] + weight_scratch,
        8 * everyone * width * mine,
        *token_slots[:1],
        tie(token_slots[1], *cot_slots[1::2]),
        *token_slots[2:],
        small[:1],
        taps,
        *weights,
    )
    branch_o, held = made[:lanes], made[lanes + 8 :]
    normed_a, b_part, c_part, x_part, conv, gated, halo, branch_y = made[lanes : lanes + 8]
    full_in, full_out = held if in_place else weights
    branch_terms = scatter(branch_o, "fsdp")
    branch_o = total(branch_terms)
    hidden_in = token_rows.astype(f32)
    second = hidden_in + branch_o
    scale_two = lax.rsqrt(jnp.mean(second * second, axis=-1, keepdims=True) + epsilon)
    unit_two = second * scale_two
    normed_u = (unit_two * small[1]).astype(bf16)

    down_rows = down_rows.reshape(width, hid).T
    full_down = tie(jnp.pad(down_rows, pad), gate_up, normed_a)
    full_down = lax.all_gather(full_down, ("fsdp", "core"), axis=0)

    u_slots = gather(normed_u, "line")
    some, half_rows = blocks // 2, line // 2 * rows
    third = lambda k: pl.BlockSpec((some, units, width), lambda j: (j, k, 0))
    half = (2, half_rows, some * units)
    per_half = pl.BlockSpec((1,) + half[1:], lambda j: (j, 0, 0))
    slot_specs = [whole((rows, width))] * line
    unit_flops = 2 * line * rows * blocks * units * width
    dhidden = kernel_call(
        functools.partial(hidden_gradient, line),
        (2,),
        slot_specs + [third(0)],
        [(half, f32, per_half)] * 2,
        [],
        unit_flops,
        *cot_slots,
        full_down,
    )
    done, du_terms = [None, None], [None] * line
    u_slots[1] = tie(u_slots[1], *dhidden)
    for odd in (1, 0):
        made = kernel_call(
            functools.partial(feed_forward, line // 2),
            (2,),
            slot_specs[: line // 2] + [third(0), third(1), per_half],
            [(half, bf16, per_half)] * 3 + flat(rows, line // 2),
            [pltpu.VMEM((half_rows, width), f32)],
            2 * unit_flops,
            *u_slots[odd::2],
            gate_up,
            gate_up,
            dhidden[odd],
        )
        done[odd] = made[:3]
        du_terms[odd::2] = made[3:]
    du_terms = scatter(du_terms, "line")
    (g_ff,) = kernel_call(
        functools.partial(feed_forward_grads, line),
        (2,),
        slot_specs * 2 + [per_half] * 6,
        [((blocks, 3 * units, width), bf16, pl.BlockSpec((some, 3 * units, width), lambda j: (j, 0, 0)))],
        [pltpu.VMEM((2, half_rows, width), bf16)] * 2,
        3 * unit_flops,
        *u_slots,
        *cot_slots,
        *done[0],
        *done[1],
    )
    g_ff = lax.psum_scatter(tie(g_ff, *du_terms[1::2]), ("fsdp", "core"), scatter_dimension=0)
    part_out = kernel_call(
        functools.partial(feed_forward_out, line),
        (2,),
        [per_half, per_half, third(0)],
        flat(rows, line),
        [pltpu.VMEM((line * rows, width), f32)],
        unit_flops,
        done[0][0],
        done[1][0],
        full_down,
    )
    dunit = total([tie(du_terms[0], part_out[0])] + du_terms[1:])
    out_terms = scatter([part_out[0]] + [tie(p, *du_terms[1:]) for p in part_out[1:]], "line")

    grad_two = jnp.sum(dunit * unit_two, axis=0)
    dnorm_two = dunit * small[1]
    dsecond = cot_rows.astype(f32) + scale_two * (
        dnorm_two - unit_two * jnp.mean(dnorm_two * unit_two, axis=-1, keepdims=True)
    )
    dbranch = dsecond.astype(bf16)
    branch_slots = gather(dbranch, "fsdp")
    everyone = lanes * rows
    dconv, dc_part = kernel_call(
        functools.partial(mixer_backward_one, lanes),
        (lanes,),
        [whole((rows, width))] * lanes + [whole((width, mine)), slot(rows, mine), slot(rows, mine)],
        [per_slot(f32, rows, mine), per_slot(bf16, rows, mine)],
        [pltpu.VMEM((rows, width), bf16)],
        2 * everyone * width * mine,
        *branch_slots,
        full_out,
        c_part,
        conv,
    )
    block_out = second + total([tie(out_terms[0], dconv)] + out_terms[1:])
    block_out = block_out.astype(bf16).reshape(seqs, group, width)
    ahead = dconv.reshape(lanes, seqs, group, mine)[:, :, :2]
    ahead = lax.ppermute(ahead, ("line", "core"), back).reshape(lanes, 2 * seqs, mine)
    *dnormed, g_mixer = kernel_call(
        functools.partial(mixer_backward_two, seqs, group, pieces, lanes),
        (lanes,),
        [whole((more, width))] * lanes
        + [whole((rows, width))] * lanes
        + [
            slot(rows, mine),
            slot(2 * seqs, mine),
            slot(rows, mine),
            slot(rows, mine),
            slot(rows, mine),
            slot(rows, mine),
            slot(more - rows, mine),
            whole((3, mine)),
            whole((1, width)),
            whole((3, mine, width)),
            whole((lanes, rows, width)),
            whole((lanes, rows, mine)),
        ],
        flat(rows, lanes)
        + [((pieces, 4 * feats + 16, width), bf16, whole((pieces, 4 * feats + 16, width)))],
        [
            pltpu.VMEM((3, lanes, rows, mine), bf16),
            pltpu.VMEM((1, width), f32),
            pltpu.VMEM((3, mine), f32),
            pltpu.VMEM((more, width), bf16),
        ],
        14 * everyone * width * mine,
        *token_slots,
        *branch_slots,
        tie(dconv, *out_terms[1:]),
        ahead,
        dc_part,
        b_part,
        x_part,
        gated,
        halo,
        taps,
        grad_two[None],
        full_in,
        normed_a,
        branch_y,
    )
    dnormed = total(scatter(dnormed, "fsdp"))
    scale_one = lax.rsqrt(jnp.mean(hidden_in * hidden_in, axis=-1, keepdims=True) + epsilon)
    unit_one = hidden_in * scale_one
    dnorm_one = dnormed * small[0]
    dinput = dsecond + scale_one * (
        dnorm_one - unit_one * jnp.mean(dnorm_one * unit_one, axis=-1, keepdims=True)
    )
    grad_tokens = dinput.astype(bf16).reshape(seqs, group, width)

    g_mixer = lax.psum_scatter(g_mixer, ("line", "core"), scatter_dimension=0)
    g_down = g_ff[2 * units : 2 * units + hid].T.reshape(count, feats, hid)
    g_down = lax.all_to_all(g_down, every, 0, 0, tiled=True)
    g_mixer = tie(g_mixer, g_down)
    g_in = g_mixer[: 3 * feats].reshape(3, feats, width)
    homes = [[(d, k) for k, d in route] for route in routes]
    parts = []
    for j in range(3):
        p = ((j - index) * pow(count, -1, 3)) % 3
        block = lax.dynamic_index_in_dim(g_in, p, 0, keepdims=False)
        parts.append(lax.ppermute(block, every, homes[j]))
    grad_in = jnp.concatenate(parts, 0).T.astype(f32)
    g_out = g_mixer[3 * feats : 4 * feats].reshape(feats, lanes, mine).transpose(1, 0, 2)
    gains = g_mixer[4 * feats : 4 * feats + 2].reshape(2, lanes, pieces, feats)
    gains = lax.dynamic_index_in_dim(gains, s_index, 2, keepdims=False).transpose(1, 0, 2)
    gains = jnp.pad(gains, ((0, 0), (0, 14), (0, mine - feats)))
    got = jnp.stack(exchange(jnp.concatenate([g_out, gains], 1), "fsdp"))
    grad_out = got[:, :feats].transpose(0, 2, 1).reshape(width, feats).astype(f32)
    gains = jnp.sum(got[:, feats : feats + 2, :feats].astype(f32), axis=0)
    grad_taps = g_mixer[4 * feats + 2 : 4 * feats + 5, :mine].reshape(3, pieces, feats)
    grad_taps = lax.dynamic_index_in_dim(grad_taps, s_index, 1, keepdims=False).astype(f32)
    grad_gate = g_ff[:hid].T.astype(f32)
    grad_up = g_ff[units : units + hid].T.astype(f32)
    grad_down = g_down.transpose(0, 2, 1).reshape(count * hid, feats).astype(f32)
    return (
        block_out,
        grad_tokens,
        gains[0],
        gains[1],
        grad_taps,
        grad_in,
        grad_out,
        grad_gate,
        grad_up,
        grad_down,
    )


def solution(mesh):
    lanes, pieces = mesh.devices.shape
    fine = Mesh(mesh.devices.reshape(lanes, pieces // 2, 2), every)
    token = P("fsdp", ("line", "core"), None)
    vector = P(every)
    columns = P(None, every)
    return jax.shard_map(
        on_device,
        mesh=fine,
        in_specs=(token, vector, vector) + (columns,) * 6 + (token,),
        out_specs=(token, token, vector, vector) + (columns,) * 6,
        check_vma=False,
    )
```

```python
import functools

import jax
import jax.numpy as jnp
from jax import lax
from jax.experimental import pallas as pl
from jax.experimental.pallas import tpu as pltpu
from jax.sharding import Mesh, PartitionSpec as P

epsilon = 1e-05
every = ("fsdp", "line", "core")
bf16 = jnp.bfloat16
f32 = jnp.float32
vmem_bytes = 58 * 2**20


def dot(left, right):
    return jnp.dot(left, right, preferred_element_type=f32)


def dot_nt(left, right):
    return lax.dot_general(left, right, (((1,), (1,)), ((), ())), preferred_element_type=f32)


def dot_tn(left, right):
    return lax.dot_general(left, right, (((0,), (0,)), ((), ())), preferred_element_type=f32)


def tie(block, *earlier):
    anywhere = pl.BlockSpec(memory_space=pl.ANY)
    return pl.pallas_call(
        lambda *refs: None,
        in_specs=[anywhere] * (1 + len(earlier)),
        out_specs=anywhere,
        out_shape=jax.ShapeDtypeStruct(block.shape, block.dtype),
        input_output_aliases={0: 0},
    )(block, *earlier)


def flip(block, axis, bits):
    size = lax.axis_size(axis)
    return lax.ppermute(block, axis, [(i, i ^ bits) for i in range(size)])


def gather(block, axis):
    return [block] + [flip(block, axis, r) for r in range(1, lax.axis_size(axis))]


def scatter(slots, axis):
    return [slots[0]] + [flip(slots[r], axis, r) for r in range(1, lax.axis_size(axis))]


def total(terms):
    return sum(t.astype(f32) for t in terms)


def exchange(blocks, axis):
    size = lax.axis_size(axis)
    me = lax.axis_index(axis)
    came = []
    for r in range(size):
        sent = lax.dynamic_index_in_dim(blocks, me ^ r, 0, keepdims=False)
        came.append(flip(sent, axis, r) if r else sent)
    out = []
    for d in range(size):
        block = came[0]
        for r in range(1, size):
            block = jnp.where(me ^ r == d, came[r], block)
        out.append(block)
    return out


def whole(shape):
    return pl.BlockSpec(shape, lambda *_: (0,) * len(shape))


def kernel_call(body, grid, ins, outs, scratch, flops, *args, waits=()):
    held = len(args)
    shapes = [jax.ShapeDtypeStruct(shape, dtype) for shape, dtype, _ in outs]
    moved = sum(a.size * a.dtype.itemsize for a in args)
    moved = (moved + sum(s.size * s.dtype.itemsize for s in shapes)) * (flops > 0)
    return pl.pallas_call(
        lambda *refs: body(*refs[:held], *refs[held + len(waits) :]),
        grid=grid,
        in_specs=ins + [pl.BlockSpec(memory_space=pl.ANY)] * len(waits),
        out_specs=[spec for _, _, spec in outs],
        out_shape=shapes,
        scratch_shapes=scratch,
        compiler_params=pltpu.CompilerParams(
            dimension_semantics=("arbitrary",) * len(grid), vmem_limit_bytes=vmem_bytes
        ),
        cost_estimate=pl.CostEstimate(flops=flops, bytes_accessed=moved, transcendentals=0),
    )(*args, *waits)


def shifted(block, distance, edge):
    rows = block.shape[0]
    moved = pltpu.roll(block, distance % rows, 0)
    row = lax.broadcasted_iota(jnp.int32, block.shape, 0)
    for n in range(abs(distance)):
        at = n if distance > 0 else rows - abs(distance) + n
        moved = jnp.where(row == at, edge[n : n + 1], moved)
    return moved


def mixer_forward(seqs, group, lanes, line, in_place, *refs):
    tok_refs, refs = refs[:lanes], refs[lanes:]
    if in_place:
        places_ref, source_refs, other, refs = refs[0], refs[1 : 1 + line], refs[1 + line], refs[2 + line :]
        source_refs = list(source_refs) + [other.at[r] for r in range(line)]
        win_ref, wout_ref = refs[lanes + 9 : lanes + 11]
        bring_weights(2 * line, places_ref, source_refs, win_ref, wout_ref, *refs[-2:])
    else:
        (added_ref, taps_ref, win_ref, wout_ref), refs = refs[:4], refs[4:]
    part_refs, refs = refs[:lanes], refs[lanes:]
    norm_ref, b_ref, c_ref, x_ref, conv_ref, gated_ref, halo_ref, y_ref, small_ref = refs[:9]
    tok_ref = refs[11 if in_place else 9]

    @pl.when(pl.program_id(0) == 0)
    def _():
        if in_place:
            small_ref[...] = sum(refs[-2][k].astype(f32) for k in range(2 * line))
        else:
            small_ref[...] = added_ref[...]

    gain_ref = small_ref.at[0:1]
    if in_place:
        mine = wout_ref.shape[1]
        at = pl.multiple_of(places_ref[2 * line] * mine, 128)
        taps_ref = small_ref.at[2:5, pl.ds(at, mine)]
    pick(tok_refs, tok_ref)
    rows = seqs * group
    h = tok_ref[...].astype(f32)
    unit = h * lax.rsqrt(jnp.mean(h * h, axis=-1, keepdims=True) + epsilon)
    norm = (unit * gain_ref[...]).astype(bf16)
    norm_ref[0] = norm[:rows]
    b_all, x_all = dot_nt(norm, win_ref[0]), dot_nt(norm, win_ref[2])
    c_part = dot_nt(norm[:rows], win_ref[1])
    b_ref[0], c_ref[0], x_ref[0] = b_all[:rows], c_part, x_all[:rows]
    gated = (b_all * x_all).astype(bf16)
    gated_ref[0], halo_ref[0] = gated[:rows], gated[rows:]
    halo = gated[rows:].astype(f32)
    for q in range(seqs):
        at = slice(q * group, (q + 1) * group)
        now = gated[at].astype(f32)
        edge = halo[2 * q : 2 * q + 2]
        conv = (
            taps_ref[0:1] * shifted(now, 2, edge)
            + taps_ref[1:2] * shifted(now, 1, edge[1:])
            + taps_ref[2:3] * now
        )
        conv_ref[0, at] = conv
        y_ref[0, at] = (c_part[at] * conv).astype(bf16)
    hand(dot_nt(y_ref[0], wout_ref[...]).astype(bf16), part_refs)


def merged(ref):
    n, units, width = ref.shape
    return ref[...].reshape(n * units, width)


def hidden_gradient(n, *refs):
    cot_refs, down_ref, out_ref = refs[:n], refs[n], refs[n + 1]
    w_down = merged(down_ref)
    rows = cot_refs[0].shape[0]
    for r in range(n):
        out_ref[0, r * rows : (r + 1) * rows] = dot_nt(cot_refs[r][...], w_down)


def add_up(acc_ref, at, part, out_ref):
    j = pl.program_id(0)

    @pl.when(j == 0)
    def _():
        acc_ref[at] = part

    @pl.when(j == 1)
    def _():
        out_ref[...] = (acc_ref[at] + part).astype(bf16)


def feed_forward(n, *refs):
    u_refs, (gate_ref, up_ref, dh_ref), refs = refs[:n], refs[n : n + 3], refs[n + 3 :]
    (hid_ref, dg_ref, dup_ref), du_refs, acc_ref = refs[:3], refs[3 : 3 + n], refs[3 + n]
    w_gate, w_up = merged(gate_ref), merged(up_ref)
    rows = u_refs[0].shape[0]
    for r in range(n):
        at = slice(r * rows, (r + 1) * rows)
        gate = dot_nt(u_refs[r][...], w_gate)
        up = dot_nt(u_refs[r][...], w_up)
        dh = dh_ref[0, at]
        sig = jax.nn.sigmoid(gate)
        silu = gate * sig
        hid_ref[0, at] = (silu * up).astype(bf16)
        dgate = (dh * up * sig * (1.0 + gate * (1.0 - sig))).astype(bf16)
        dup = (dh * silu).astype(bf16)
        dg_ref[0, at] = dgate
        dup_ref[0, at] = dup
        add_up(acc_ref, at, dot(dgate, w_gate) + dot(dup, w_up), du_refs[r])


def feed_forward_out(line, *refs):
    hid_refs, down_ref, out_refs, acc_ref = refs[:2], refs[2], refs[3 : 3 + line], refs[3 + line]
    w_down = merged(down_ref)
    rows = out_refs[0].shape[0]
    for r in range(line):
        part = dot(hid_refs[r % 2][0, r // 2 * rows : (r // 2 + 1) * rows], w_down)
        add_up(acc_ref, slice(r * rows, (r + 1) * rows), part, out_refs[r])


def feed_forward_grads(line, kinds, *refs):
    right_refs, halves, refs = refs[:line], refs[line : line + 2 * kinds], refs[line + 2 * kinds :]
    out_ref, right_all = refs
    rows = right_refs[0].shape[0]

    @pl.when(pl.program_id(0) == 0)
    def _():
        for r in range(line):
            right_all[r % 2, r // 2 * rows : (r // 2 + 1) * rows] = right_refs[r][...]

    n, units, width = out_ref.shape
    units //= kinds
    for k in range(kinds):
        part = sum(dot_tn(halves[h * kinds + k][0], right_all[h]) for h in range(2))
        out_ref[:, k * units : (k + 1) * units] = part.astype(bf16).reshape(n, units, width)


def pick(slot_refs, out_ref):
    for r, ref in enumerate(slot_refs):

        @pl.when(pl.program_id(0) == r)
        def _(ref=ref):
            out_ref[...] = ref[...]


def hand(block, out_refs):
    for r, ref in enumerate(out_refs):

        @pl.when(pl.program_id(0) == r)
        def _(ref=ref):
            ref[...] = block


def bring_weights(pieces, places_ref, sources, win_ref, wout_ref, small_ref, sems):
    width, mine = wout_ref.shape
    feats = mine // pieces
    copies = []
    for k, source in enumerate(sources):
        s = places_ref[k]
        for p in range(3):
            rows = pl.ds(pl.multiple_of(s * feats, 16), feats)
            copies.append((source.at[pl.ds(p * feats, feats)], win_ref.at[p, rows]))
        for f in range(width // mine):
            rows = pl.ds(pl.multiple_of((f * pieces + s) * feats, 16), feats)
            columns = source.at[pl.ds(3 * feats, feats), pl.ds(f * mine, mine)]
            copies.append((columns, wout_ref.at[rows]))
        copies.append((source.at[pl.ds(4 * feats, 16)], small_ref.at[k]))
    copies = [pltpu.make_async_copy(a, b, sems.at[n]) for n, (a, b) in enumerate(copies)]

    @pl.when(pl.program_id(0) == 0)
    def _():
        for copy in copies:
            copy.start()
        for copy in copies:
            copy.wait()


def mixer_backward_one(lanes, *refs):
    branch_refs, (wout_ref, c_ref, conv_ref, dconv_ref, dc_ref, now_ref) = refs[:lanes], refs[lanes:]
    pick(branch_refs, now_ref)
    dy = dot(now_ref[...], wout_ref[...])
    dconv_ref[0] = dy * c_ref[0]
    dc_ref[0] = (dy * conv_ref[0]).astype(bf16)


def mixer_backward_two(seqs, group, pieces, lanes, in_place, *refs):
    tok_refs, branch_refs, refs = refs[:lanes], refs[lanes : 2 * lanes], refs[2 * lanes :]
    (dconv_ref, ahead_ref, dc_ref, b_ref, x_ref, gated_ref, halo_ref, taps_ref, two_ref) = refs[:9]
    (win_ref, norm_ref, y_ref, places_ref), refs = refs[9:13], refs[13:]
    part_refs, out_refs, refs = refs[:lanes], refs[lanes : lanes + 2], refs[lanes + 2 :]
    dm_ref, one_ref, dt_ref, tok_ref, gin_ref, gout_ref = refs
    pick(tok_refs, tok_ref)
    r = pl.program_id(0)
    rows = seqs * group
    width = norm_ref.shape[2]
    mine = win_ref.shape[1]

    @pl.when(r == 0)
    def _():
        one_ref[...] = jnp.zeros_like(one_ref)
        dt_ref[...] = jnp.zeros_like(dt_ref)

    for q in range(seqs):
        at = slice(q * group, (q + 1) * group)
        now = dconv_ref[0, at]
        edge = ahead_ref[0, 2 * q : 2 * q + 2]
        dgated = (
            taps_ref[2:3] * now
            + taps_ref[1:2] * shifted(now, -1, edge)
            + taps_ref[0:1] * shifted(now, -2, edge)
        )
        dm_ref[0, r, at] = (dgated * x_ref[0, at]).astype(bf16)
        dm_ref[2, r, at] = (dgated * b_ref[0, at]).astype(bf16)
        held = gated_ref[0, at].astype(f32)
        past = halo_ref[0].astype(f32)[2 * q : 2 * q + 2]
        for k, block in enumerate((shifted(held, 2, past), shifted(held, 1, past[1:]), held)):
            dt_ref[k : k + 1] += jnp.sum(now * block, axis=0, keepdims=True)
    dm_ref[1, r] = dc_ref[0]
    da = sum(dot(dm_ref[p, r], win_ref[p]) for p in range(3))
    hand(da.astype(bf16), part_refs)
    h = tok_ref[:rows].astype(f32)
    unit = h * lax.rsqrt(jnp.mean(h * h, axis=-1, keepdims=True) + epsilon)
    one_ref[...] += jnp.sum(da * unit, axis=0, keepdims=True)

    @pl.when(r == pl.num_programs(0) - 1)
    def _():
        slots = norm_ref.shape[0]
        feats = mine // pieces
        norm = norm_ref[...].reshape(slots * rows, width)
        for p in range(3):
            gin_ref[p] = dot_tn(dm_ref[p].reshape(slots * rows, mine), norm).astype(bf16)
        g_out = sum(dot_tn(branch_refs[f][...], y_ref[f]) for f in range(lanes))
        gout_ref[...] = g_out.astype(bf16)
        small = jnp.concatenate([one_ref[...], two_ref[...], jnp.zeros((14, width), f32)], 0)
        small = small.astype(bf16)
        for n in range(pieces):
            out_ref, k = out_refs[n * 2 // pieces], n % (pieces // 2)
            s = pl.multiple_of(places_ref[n] * feats, 16) if in_place else n * feats
            for p in range(3):
                out_ref[k, p * feats : (p + 1) * feats] = gin_ref[p, pl.ds(s, feats)]
            for f in range(lanes):
                at = pl.ds(f * pieces * feats + s, feats)
                out_ref[k, 3 * feats : 4 * feats, f * mine : (f + 1) * mine] = gout_ref[at]
            out_ref[k, 4 * feats :] = small
            out_ref[k, 4 * feats + 2 : 4 * feats + 5, :mine] = dt_ref[...].astype(bf16)


def add_cores(*refs):
    own_ref, came_ref, out_refs = refs[0], refs[1], refs[2:]
    for r, out_ref in enumerate(out_refs):
        out_ref[...] = (own_ref[r].astype(f32) + came_ref[r].astype(f32)).astype(bf16)


def on_device(tokens, gain_one, gain_two, conv_taps, w_in, w_out, w_gate, w_up, w_down, cotangent):
    seqs, group, width = tokens.shape
    rows = seqs * group
    lanes, line = lax.axis_size("fsdp"), lax.axis_size("line")
    pieces = 2 * line
    count = lanes * pieces
    feats = width // count
    mine = width // lanes
    hid = w_gate.shape[1]
    units = -(-hid // 16) * 16
    blocks = lanes * 2
    f_index = lax.axis_index("fsdp")
    s_index = lax.axis_index(("line", "core"))
    index = lax.axis_index(every)
    onward = [(i, i + 1) for i in range(pieces - 1)]
    back = [(i + 1, i) for i in range(pieces - 1)]

    in_blocks = w_in.T.reshape(3, feats, width)
    routes = [[(k, (3 * k + j) % count) for k in range(count)] for j in range(3)]
    came = jnp.stack([lax.ppermute(in_blocks[j], every, routes[j]) for j in range(3)])
    in_parts = [
        lax.dynamic_index_in_dim(came, (index + p * count) % 3, 0, keepdims=False) for p in range(3)
    ]
    smalls = jnp.pad(jnp.concatenate([gain_one[None], gain_two[None], conv_taps], 0), ((0, 11), (0, 0)))
    smalls = lax.dynamic_update_slice(jnp.zeros((16, mine), bf16), smalls, (0, s_index * feats))
    out_blocks = w_out.T.reshape(feats, lanes, mine).transpose(1, 0, 2)
    out_blocks = jnp.concatenate([out_blocks, jnp.broadcast_to(smalls, (lanes, 16, mine))], 1)
    out_blocks = jnp.concatenate(exchange(out_blocks, "fsdp"), 1)
    edge = lax.ppermute(tokens[:, group - 2 :], ("line", "core"), onward).reshape(2 * seqs, width)
    edge = jnp.pad(edge, ((0, -2 * seqs % 16), (0, 0)))
    mixer_own = tie(jnp.concatenate(in_parts + [out_blocks], 0), edge)
    mixer_slots = gather(mixer_own, "line")
    token_rows = tokens.reshape(rows, width)
    token_slots = gather(tie(jnp.concatenate([token_rows, edge], 0), mixer_own), "fsdp")

    down_rows = tie(w_down.T.reshape(feats, count, hid).transpose(1, 0, 2), mixer_own)
    down_rows = lax.all_to_all(down_rows, every, 0, 0, tiled=True)

    swapped = tie(jnp.stack(mixer_slots), *token_slots[1:], down_rows)
    swapped = flip(swapped, "core", 1)
    cot_rows = cotangent.reshape(rows, width)
    cot_slots = gather(tie(cot_rows, *mixer_slots[1:]), "line")
    z_index, c_index = lax.axis_index("line"), lax.axis_index("core")
    near = [r ^ z_index for r in range(line)]
    places = [2 * z + c_index for z in near]
    places += [2 * z + 1 - c_index for z in near]
    places = jnp.stack(places + [f_index]).astype(jnp.int32)
    anywhere = pl.BlockSpec(memory_space=pl.ANY)
    in_place = feats % 16 == 0 and mine % 128 == 0
    if in_place:
        weights = [places] + mixer_slots + [swapped]
        weight_specs = [pl.BlockSpec(memory_space=pltpu.SMEM)] + [anywhere] * (line + 1)
        weight_outs = [((3, mine, width), bf16, whole((3, mine, width)))]
        weight_outs += [((width, mine), bf16, whole((width, mine)))]
        weight_scratch = [
            pltpu.VMEM((pieces, 16, width), bf16),
            pltpu.SemaphoreType.DMA((pieces * (4 + lanes),)),
        ]
    else:
        mixer_w = jnp.concatenate([jnp.stack(mixer_slots), swapped], 0)[jnp.argsort(places[:-1])]
        full_in = mixer_w[:, : 3 * feats].reshape(pieces, 3, feats, width)
        full_in = full_in.transpose(1, 0, 2, 3).reshape(3, mine, width)
        full_out = mixer_w[:, 3 * feats : 4 * feats].reshape(pieces, feats, lanes, mine)
        full_out = full_out.transpose(2, 0, 1, 3).reshape(width, mine)
        small = jnp.sum(mixer_w[:, 4 * feats :].astype(f32), axis=0)
        taps = lax.dynamic_slice_in_dim(small[2:5], f_index * mine, mine, 1)
        weights = [small, taps, full_in, full_out]
        weight_specs = [whole((16, width)), whole((3, mine))]
        weight_specs += [whole((3, mine, width)), whole((width, mine))]
        weight_outs = weight_scratch = []

    pad = ((0, units - hid), (0, 0))
    gate_up = jnp.concatenate([jnp.pad(w, pad) for w in (w_gate.T, w_up.T)], 0)
    gate_up = lax.all_gather(gate_up, ("fsdp", "core"), axis=0)

    more = token_slots[0].shape[0]
    everyone = lanes * rows
    slot = lambda *shape: pl.BlockSpec((1,) + shape, lambda r: (r,) + (0,) * len(shape))
    per_slot = lambda dtype, *shape: ((lanes,) + shape, dtype, slot(*shape))
    flat = lambda n, count: [((n, width), bf16, whole((n, width)))] * count
    made = kernel_call(
        functools.partial(mixer_forward, seqs, group, lanes, line, in_place),
        (lanes,),
        [whole((more, width))] * lanes + weight_specs,
        flat(rows, lanes)
        + [per_slot(bf16, rows, width)]
        + [per_slot(f32, rows, mine)] * 4
        + [per_slot(bf16, rows, mine), per_slot(bf16, more - rows, mine), per_slot(bf16, rows, mine)]
        + [((16, width), f32, whole((16, width)))]
        + weight_outs,
        [pltpu.VMEM((more, width), bf16)] + weight_scratch,
        24 * everyone * width * mine,
        *token_slots,
        *weights,
    )
    branch_o, held = list(made[:lanes]), made[lanes + 9 :]
    normed_a, b_part, c_part, x_part, conv, gated, halo, branch_y, small = made[lanes : lanes + 9]
    full_in, full_out = held if in_place else weights[2:]
    taps = lax.dynamic_slice_in_dim(small[2:5], f_index * mine, mine, 1)
    branch_o[1] = tie(branch_o[1], cot_slots[-1])
    branch_terms = scatter(branch_o, "fsdp")
    branch_o = total(branch_terms)
    hidden_in = token_rows.astype(f32)
    second = hidden_in + branch_o
    scale_two = lax.rsqrt(jnp.mean(second * second, axis=-1, keepdims=True) + epsilon)
    unit_two = second * scale_two
    normed_u = (unit_two * small[1]).astype(bf16)

    down_rows = down_rows.reshape(width, hid).T
    full_down = tie(jnp.pad(down_rows, pad), gate_up, swapped)
    full_down = lax.all_gather(full_down, ("fsdp", "core"), axis=0)

    some, half_rows = blocks // 2, line // 2 * rows
    third = lambda k: pl.BlockSpec((some, units, width), lambda j: (j, k, 0))
    half = (2, half_rows, some * units)
    per_half = pl.BlockSpec((1,) + half[1:], lambda j: (j, 0, 0))
    slot_specs = [whole((rows, width))] * line
    unit_flops = 2 * line * rows * blocks * units * width
    dhidden = [
        kernel_call(
            functools.partial(hidden_gradient, line // 2),
            (2,),
            slot_specs[: line // 2] + [third(0)],
            [(half, f32, per_half)],
            [],
            unit_flops // 2,
            *cot_slots[odd::2],
            full_down,
        )[0]
        for odd in range(2)
    ]
    normed_u = tie(normed_u, *cot_slots[2::2])
    u_slots = [normed_u] + [None] * (line - 1)
    for r in range(1, line, 2):
        u_slots[r] = flip(normed_u, "line", r)
    held_back = tie(normed_u, *u_slots[1::2], dhidden[1])
    for r in range(2, line, 2):
        u_slots[r] = flip(held_back, "line", r)
    done, du_terms = [None, None], [None] * line
    for odd in (1, 0):
        made = kernel_call(
            functools.partial(feed_forward, line // 2),
            (2,),
            slot_specs[: line // 2] + [third(0), third(1), per_half],
            [(half, bf16, per_half)] * 3 + flat(rows, line // 2),
            [pltpu.VMEM((half_rows, width), f32)],
            2 * unit_flops,
            *u_slots[odd::2],
            gate_up,
            gate_up,
            dhidden[odd],
            waits=[] if odd else [done[1][0]],
        )
        done[odd] = made[:3]
        du_terms[odd::2] = made[3:]
    du_terms = scatter(du_terms, "line")
    ff_grads = lambda kinds, *args: kernel_call(
        functools.partial(feed_forward_grads, line, kinds),
        (2,),
        slot_specs + [per_half] * (2 * kinds),
        [
            (
                (blocks, kinds * units, width),
                bf16,
                pl.BlockSpec((some, kinds * units, width), lambda j: (j, 0, 0)),
            )
        ],
        [pltpu.VMEM((2, half_rows, width), bf16)],
        kinds * unit_flops,
        *args,
    )[0]
    g_down = ff_grads(1, *cot_slots, done[0][0], done[1][0])
    g_ff = ff_grads(2, *u_slots, *done[0][1:], *done[1][1:])
    part_out = kernel_call(
        functools.partial(feed_forward_out, line),
        (2,),
        [per_half, per_half, third(0)],
        flat(rows, line),
        [pltpu.VMEM((line * rows, width), f32)],
        unit_flops,
        done[0][0],
        done[1][0],
        full_down,
    )
    dunit = total([tie(du_terms[0], part_out[0])] + du_terms[1:])
    out_terms = scatter([part_out[0]] + [tie(p, *du_terms[1:]) for p in part_out[1:]], "line")

    grad_two = jnp.sum(dunit * unit_two, axis=0)
    dnorm_two = dunit * small[1]
    dsecond = cot_rows.astype(f32) + scale_two * (
        dnorm_two - unit_two * jnp.mean(dnorm_two * unit_two, axis=-1, keepdims=True)
    )
    dbranch = dsecond.astype(bf16)
    branch_slots = gather(dbranch, "fsdp")
    everyone = lanes * rows
    dconv, dc_part = kernel_call(
        functools.partial(mixer_backward_one, lanes),
        (lanes,),
        [whole((rows, width))] * lanes + [whole((width, mine)), slot(rows, mine), slot(rows, mine)],
        [per_slot(f32, rows, mine), per_slot(bf16, rows, mine)],
        [pltpu.VMEM((rows, width), bf16)],
        2 * everyone * width * mine,
        *branch_slots,
        full_out,
        c_part,
        conv,
        waits=out_terms[1:-1] + [g_ff],
    )
    g_down = lax.psum_scatter(tie(g_down, dconv), ("fsdp", "core"), scatter_dimension=0)
    block_out = second + total([tie(out_terms[0], dconv)] + out_terms[1:])
    block_out = block_out.astype(bf16).reshape(seqs, group, width)
    ahead = dconv.reshape(lanes, seqs, group, mine)[:, :, :2]
    ahead = lax.ppermute(ahead, ("line", "core"), back).reshape(lanes, 2 * seqs, mine)
    g_rows = 4 * feats + 16
    *dnormed, g_own, g_other = kernel_call(
        functools.partial(mixer_backward_two, seqs, group, pieces, lanes, in_place),
        (lanes,),
        [whole((more, width))] * lanes
        + [whole((rows, width))] * lanes
        + [
            slot(rows, mine),
            slot(2 * seqs, mine),
            slot(rows, mine),
            slot(rows, mine),
            slot(rows, mine),
            slot(rows, mine),
            slot(more - rows, mine),
            whole((3, mine)),
            whole((1, width)),
            whole((3, mine, width)),
            whole((lanes, rows, width)),
            whole((lanes, rows, mine)),
            pl.BlockSpec(memory_space=pltpu.SMEM),
        ],
        flat(rows, lanes)
        + [((line, g_rows, width), bf16, whole((line, g_rows, width)))] * 2,
        [
            pltpu.VMEM((3, lanes, rows, mine), bf16),
            pltpu.VMEM((1, width), f32),
            pltpu.VMEM((3, mine), f32),
            pltpu.VMEM((more, width), bf16),
            pltpu.VMEM((3, mine, width), bf16),
            pltpu.VMEM((width, mine), bf16),
        ],
        14 * everyone * width * mine,
        *token_slots,
        *branch_slots,
        dconv,
        ahead,
        dc_part,
        b_part,
        x_part,
        gated,
        halo,
        taps,
        grad_two[None],
        full_in,
        normed_a,
        branch_y,
        places,
    )
    if not in_place:
        g_mixer = jnp.concatenate([g_own, g_other], 0)[places[:-1]]
        g_own, g_other = g_mixer[:line], g_mixer[line:]
    g_terms = kernel_call(
        add_cores,
        (1,),
        [whole((line, g_rows, width))] * 2,
        flat(g_rows, line),
        [],
        1,
        g_own,
        flip(g_other, "core", 1),
    )
    g_ff = tie(g_ff, g_other, out_terms[-1])
    g_ff = lax.psum_scatter(g_ff, ("fsdp", "core"), scatter_dimension=0)
    dnormed = [dnormed[0]] + [tie(d, g_terms[0]) for d in dnormed[1:]]
    g_terms = scatter(g_terms, "line")
    da_terms = scatter(dnormed, "fsdp")
    g_down = g_down[:hid].T.reshape(count, feats, hid)
    ready = g_down
    g_down = lax.all_to_all(g_down, every, 0, 0, tiled=True)
    dnormed = total(da_terms)
    scale_one = lax.rsqrt(jnp.mean(hidden_in * hidden_in, axis=-1, keepdims=True) + epsilon)
    unit_one = hidden_in * scale_one
    dnorm_one = dnormed * small[0]
    dinput = dsecond + scale_one * (
        dnorm_one - unit_one * jnp.mean(dnorm_one * unit_one, axis=-1, keepdims=True)
    )
    grad_tokens = dinput.astype(bf16).reshape(seqs, group, width)

    g_mixer = total([tie(g_terms[0], ready)] + g_terms[1:]).astype(bf16)
    g_in = g_mixer[: 3 * feats].reshape(3, feats, width)
    homes = [[(d, k) for k, d in route] for route in routes]
    parts = []
    for j in range(3):
        p = ((j - index) * pow(count, -1, 3)) % 3
        block = lax.dynamic_index_in_dim(g_in, p, 0, keepdims=False)
        parts.append(lax.ppermute(block, every, homes[j]))
    grad_in = jnp.concatenate(parts, 0).T.astype(f32)
    g_out = g_mixer[3 * feats : 4 * feats].reshape(feats, lanes, mine).transpose(1, 0, 2)
    gains = g_mixer[4 * feats : 4 * feats + 2].reshape(2, lanes, pieces, feats)
    gains = lax.dynamic_index_in_dim(gains, s_index, 2, keepdims=False).transpose(1, 0, 2)
    gains = jnp.pad(gains, ((0, 0), (0, 14), (0, mine - feats)))
    got = jnp.stack(exchange(jnp.concatenate([g_out, gains], 1), "fsdp"))
    grad_out = got[:, :feats].transpose(0, 2, 1).reshape(width, feats).astype(f32)
    gains = jnp.sum(got[:, feats : feats + 2, :feats].astype(f32), axis=0)
    grad_taps = g_mixer[4 * feats + 2 : 4 * feats + 5, :mine].reshape(3, pieces, feats)
    grad_taps = lax.dynamic_index_in_dim(grad_taps, s_index, 1, keepdims=False).astype(f32)
    grad_gate = g_ff[:hid].T.astype(f32)
    grad_up = g_ff[units : units + hid].T.astype(f32)
    grad_down = g_down.transpose(0, 2, 1).reshape(count * hid, feats).astype(f32)
    return (
        block_out,
        grad_tokens,
        gains[0],
        gains[1],
        grad_taps,
        grad_in,
        grad_out,
        grad_gate,
        grad_up,
        grad_down,
    )


def solution(mesh):
    lanes, pieces = mesh.devices.shape
    fine = Mesh(mesh.devices.reshape(lanes, pieces // 2, 2), every)
    token = P("fsdp", ("line", "core"), None)
    vector = P(every)
    columns = P(None, every)
    return jax.shard_map(
        on_device,
        mesh=fine,
        in_specs=(token, vector, vector) + (columns,) * 6 + (token,),
        out_specs=(token, token, vector, vector) + (columns,) * 6,
        check_vma=False,
    )
```

```python
import functools

import jax
import jax.numpy as jnp
from jax import lax
from jax.experimental import pallas as pl
from jax.experimental.pallas import tpu as pltpu
from jax.sharding import Mesh, PartitionSpec as P

epsilon = 1e-05
every = ("fsdp", "line", "core")
bf16 = jnp.bfloat16
f32 = jnp.float32
vmem_bytes = 58 * 2**20


def dot(left, right):
    return jnp.dot(left, right, preferred_element_type=f32)


def dot_nt(left, right):
    return lax.dot_general(left, right, (((1,), (1,)), ((), ())), preferred_element_type=f32)


def dot_tn(left, right):
    return lax.dot_general(left, right, (((0,), (0,)), ((), ())), preferred_element_type=f32)


def tie(block, *earlier):
    anywhere = pl.BlockSpec(memory_space=pl.ANY)
    return pl.pallas_call(
        lambda *refs: None,
        in_specs=[anywhere] * (1 + len(earlier)),
        out_specs=anywhere,
        out_shape=jax.ShapeDtypeStruct(block.shape, block.dtype),
        input_output_aliases={0: 0},
    )(block, *earlier)


def flip(block, axis, bits):
    size = lax.axis_size(axis)
    return lax.ppermute(block, axis, [(i, i ^ bits) for i in range(size)])


def gather(block, axis):
    return [block] + [flip(block, axis, r) for r in range(1, lax.axis_size(axis))]


def scatter(slots, axis):
    return [slots[0]] + [flip(slots[r], axis, r) for r in range(1, lax.axis_size(axis))]


def total(terms):
    return sum(t.astype(f32) for t in terms)


def exchange(blocks, axis):
    size = lax.axis_size(axis)
    me = lax.axis_index(axis)
    came = []
    for r in range(size):
        sent = lax.dynamic_index_in_dim(blocks, me ^ r, 0, keepdims=False)
        came.append(flip(sent, axis, r) if r else sent)
    out = []
    for d in range(size):
        block = came[0]
        for r in range(1, size):
            block = jnp.where(me ^ r == d, came[r], block)
        out.append(block)
    return out


def whole(shape):
    return pl.BlockSpec(shape, lambda *_: (0,) * len(shape))


def kernel_call(body, grid, ins, outs, scratch, flops, *args, waits=()):
    held = len(args)
    shapes = [jax.ShapeDtypeStruct(shape, dtype) for shape, dtype, _ in outs]
    moved = sum(a.size * a.dtype.itemsize for a in args)
    moved = (moved + sum(s.size * s.dtype.itemsize for s in shapes)) * (flops > 0)
    return pl.pallas_call(
        lambda *refs: body(*refs[:held], *refs[held + len(waits) :]),
        grid=grid,
        in_specs=ins + [pl.BlockSpec(memory_space=pl.ANY)] * len(waits),
        out_specs=[spec for _, _, spec in outs],
        out_shape=shapes,
        scratch_shapes=scratch,
        compiler_params=pltpu.CompilerParams(
            dimension_semantics=("arbitrary",) * len(grid), vmem_limit_bytes=vmem_bytes
        ),
        cost_estimate=pl.CostEstimate(flops=flops, bytes_accessed=moved, transcendentals=0),
    )(*args, *waits)


def shifted(block, distance, edge):
    rows = block.shape[0]
    moved = pltpu.roll(block, distance % rows, 0)
    row = lax.broadcasted_iota(jnp.int32, block.shape, 0)
    for n in range(abs(distance)):
        at = n if distance > 0 else rows - abs(distance) + n
        moved = jnp.where(row == at, edge[n : n + 1], moved)
    return moved


def mixer_forward(seqs, group, lanes, line, in_place, *refs):
    tok_refs, refs = refs[:lanes], refs[lanes:]
    if in_place:
        places_ref, source_refs, other, refs = refs[0], refs[1 : 1 + line], refs[1 + line], refs[2 + line :]
        source_refs = list(source_refs) + [other.at[r] for r in range(line)]
        win_ref, wout_ref = refs[lanes + 9 : lanes + 11]
        bring_weights(2 * line, places_ref, source_refs, win_ref, wout_ref, *refs[-2:])
    else:
        (added_ref, taps_ref, win_ref, wout_ref), refs = refs[:4], refs[4:]
    part_refs, refs = refs[:lanes], refs[lanes:]
    norm_ref, b_ref, c_ref, x_ref, conv_ref, gated_ref, halo_ref, y_ref, small_ref = refs[:9]
    tok_ref = refs[11 if in_place else 9]

    @pl.when(pl.program_id(0) == 0)
    def _():
        if in_place:
            small_ref[...] = sum(refs[-2][k].astype(f32) for k in range(2 * line))
        else:
            small_ref[...] = added_ref[...]

    gain_ref = small_ref.at[0:1]
    if in_place:
        mine = wout_ref.shape[1]
        at = pl.multiple_of(places_ref[2 * line] * mine, 128)
        taps_ref = small_ref.at[2:5, pl.ds(at, mine)]
    pick(tok_refs, tok_ref)
    rows = seqs * group
    h = tok_ref[...].astype(f32)
    unit = h * lax.rsqrt(jnp.mean(h * h, axis=-1, keepdims=True) + epsilon)
    norm = (unit * gain_ref[...]).astype(bf16)
    norm_ref[0] = norm[:rows]
    b_all, x_all = dot_nt(norm, win_ref[0]), dot_nt(norm, win_ref[2])
    c_part = dot_nt(norm[:rows], win_ref[1])
    b_ref[0], c_ref[0], x_ref[0] = b_all[:rows], c_part, x_all[:rows]
    gated = (b_all * x_all).astype(bf16)
    gated_ref[0], halo_ref[0] = gated[:rows], gated[rows:]
    halo = gated[rows:].astype(f32)
    for q in range(seqs):
        at = slice(q * group, (q + 1) * group)
        now = gated[at].astype(f32)
        edge = halo[2 * q : 2 * q + 2]
        conv = (
            taps_ref[0:1] * shifted(now, 2, edge)
            + taps_ref[1:2] * shifted(now, 1, edge[1:])
            + taps_ref[2:3] * now
        )
        conv_ref[0, at] = conv
        y_ref[0, at] = (c_part[at] * conv).astype(bf16)
    hand(dot_nt(y_ref[0], wout_ref[...]).astype(bf16), part_refs)


def merged(ref):
    n, units, width = ref.shape
    return ref[...].reshape(n * units, width)


def hidden_gradient(n, *refs):
    cot_refs, down_ref, out_ref = refs[:n], refs[n], refs[n + 1]
    w_down = merged(down_ref)
    rows = cot_refs[0].shape[0]
    for r in range(n):
        out_ref[0, r * rows : (r + 1) * rows] = dot_nt(cot_refs[r][...], w_down)


def add_up(acc_ref, at, part, out_ref):
    j = pl.program_id(0)

    @pl.when(j == 0)
    def _():
        acc_ref[at] = part

    @pl.when(j == 1)
    def _():
        out_ref[...] = (acc_ref[at] + part).astype(bf16)


def feed_forward(n, parts, *refs):
    u_refs, (gate_ref, up_ref, dh_ref), refs = refs[:n], refs[n : n + 3], refs[n + 3 :]
    (hid_ref, dg_ref, dup_ref), du_refs, acc_ref = refs[:3], refs[3:-1], refs[-1]
    w_gate, w_up = merged(gate_ref), merged(up_ref)
    rows = u_refs[0].shape[0]
    for r in range(n):
        at = slice(r * rows, (r + 1) * rows)
        gate = dot_nt(u_refs[r][...], w_gate)
        up = dot_nt(u_refs[r][...], w_up)
        dh = dh_ref[0, at]
        sig = jax.nn.sigmoid(gate)
        silu = gate * sig
        hid_ref[0, at] = (silu * up).astype(bf16)
        dgate = (dh * up * sig * (1.0 + gate * (1.0 - sig))).astype(bf16)
        dup = (dh * silu).astype(bf16)
        dg_ref[0, at] = dgate
        dup_ref[0, at] = dup
        du = dot(dgate, w_gate) + dot(dup, w_up)
        ends = [0, rows // 8, rows] if parts == 2 else [0, rows]
        for h in range(parts):
            here = slice(r * rows + ends[h], r * rows + ends[h + 1])
            add_up(acc_ref, here, du[ends[h] : ends[h + 1]], du_refs[r * parts + h])


def feed_forward_out(line, *refs):
    hid_refs, down_ref, out_refs, acc_ref = refs[:2], refs[2], refs[3 : 3 + line], refs[3 + line]
    w_down = merged(down_ref)
    rows = out_refs[0].shape[0]
    for r in range(line):
        part = dot(hid_refs[r % 2][0, r // 2 * rows : (r // 2 + 1) * rows], w_down)
        add_up(acc_ref, slice(r * rows, (r + 1) * rows), part, out_refs[r])


def feed_forward_grads(line, kinds, *refs):
    right_refs, halves, refs = refs[:line], refs[line : line + 2 * kinds], refs[line + 2 * kinds :]
    out_ref, right_all = refs
    rows = right_refs[0].shape[0]

    @pl.when(pl.program_id(0) == 0)
    def _():
        for r in range(line):
            right_all[r % 2, r // 2 * rows : (r // 2 + 1) * rows] = right_refs[r][...]

    n, units, width = out_ref.shape
    units //= kinds
    for k in range(kinds):
        part = sum(dot_tn(halves[h * kinds + k][0], right_all[h]) for h in range(2))
        out_ref[:, k * units : (k + 1) * units] = part.astype(bf16).reshape(n, units, width)


def pick(slot_refs, out_ref):
    for r, ref in enumerate(slot_refs):

        @pl.when(pl.program_id(0) == r)
        def _(ref=ref):
            out_ref[...] = ref[...]


def hand(block, out_refs):
    for r, ref in enumerate(out_refs):

        @pl.when(pl.program_id(0) == r)
        def _(ref=ref):
            ref[...] = block


def bring_weights(pieces, places_ref, sources, win_ref, wout_ref, small_ref, sems):
    width, mine = wout_ref.shape
    feats = mine // pieces
    copies = []
    for k, source in enumerate(sources):
        s = places_ref[k]
        for p in range(3):
            rows = pl.ds(pl.multiple_of(s * feats, 16), feats)
            copies.append((source.at[pl.ds(p * feats, feats)], win_ref.at[p, rows]))
        for f in range(width // mine):
            rows = pl.ds(pl.multiple_of((f * pieces + s) * feats, 16), feats)
            columns = source.at[pl.ds(3 * feats, feats), pl.ds(f * mine, mine)]
            copies.append((columns, wout_ref.at[rows]))
        copies.append((source.at[pl.ds(4 * feats, 16)], small_ref.at[k]))
    copies = [pltpu.make_async_copy(a, b, sems.at[n]) for n, (a, b) in enumerate(copies)]

    @pl.when(pl.program_id(0) == 0)
    def _():
        for copy in copies:
            copy.start()
        for copy in copies:
            copy.wait()


def mixer_backward_one(lanes, *refs):
    branch_refs, (wout_ref, c_ref, conv_ref, dconv_ref, dc_ref, now_ref) = refs[:lanes], refs[lanes:]
    pick(branch_refs, now_ref)
    dy = dot(now_ref[...], wout_ref[...])
    dconv_ref[0] = dy * c_ref[0]
    dc_ref[0] = (dy * conv_ref[0]).astype(bf16)


def mixer_backward_two(seqs, group, pieces, lanes, in_place, *refs):
    tok_refs, branch_refs, refs = refs[:lanes], refs[lanes : 2 * lanes], refs[2 * lanes :]
    (dconv_ref, ahead_ref, dc_ref, b_ref, x_ref, gated_ref, halo_ref, taps_ref, two_ref) = refs[:9]
    (win_ref, norm_ref, y_ref, places_ref), refs = refs[9:13], refs[13:]
    part_refs, out_refs, refs = refs[:lanes], refs[lanes : lanes + 2], refs[lanes + 2 :]
    dm_ref, one_ref, dt_ref, tok_ref, gin_ref, gout_ref = refs
    pick(tok_refs, tok_ref)
    r = pl.program_id(0)
    rows = seqs * group
    width = norm_ref.shape[2]
    mine = win_ref.shape[1]

    @pl.when(r == 0)
    def _():
        one_ref[...] = jnp.zeros_like(one_ref)
        dt_ref[...] = jnp.zeros_like(dt_ref)

    for q in range(seqs):
        at = slice(q * group, (q + 1) * group)
        now = dconv_ref[0, at]
        edge = ahead_ref[0, 2 * q : 2 * q + 2]
        dgated = (
            taps_ref[2:3] * now
            + taps_ref[1:2] * shifted(now, -1, edge)
            + taps_ref[0:1] * shifted(now, -2, edge)
        )
        dm_ref[0, r, at] = (dgated * x_ref[0, at]).astype(bf16)
        dm_ref[2, r, at] = (dgated * b_ref[0, at]).astype(bf16)
        held = gated_ref[0, at].astype(f32)
        past = halo_ref[0].astype(f32)[2 * q : 2 * q + 2]
        for k, block in enumerate((shifted(held, 2, past), shifted(held, 1, past[1:]), held)):
            dt_ref[k : k + 1] += jnp.sum(now * block, axis=0, keepdims=True)
    dm_ref[1, r] = dc_ref[0]
    da = sum(dot(dm_ref[p, r], win_ref[p]) for p in range(3))
    hand(da.astype(bf16), part_refs)
    h = tok_ref[:rows].astype(f32)
    unit = h * lax.rsqrt(jnp.mean(h * h, axis=-1, keepdims=True) + epsilon)
    one_ref[...] += jnp.sum(da * unit, axis=0, keepdims=True)

    @pl.when(r == pl.num_programs(0) - 1)
    def _():
        slots = norm_ref.shape[0]
        feats = mine // pieces
        norm = norm_ref[...].reshape(slots * rows, width)
        for p in range(3):
            gin_ref[p] = dot_tn(dm_ref[p].reshape(slots * rows, mine), norm).astype(bf16)
        g_out = sum(dot_tn(branch_refs[f][...], y_ref[f]) for f in range(lanes))
        gout_ref[...] = g_out.astype(bf16)
        small = jnp.concatenate([one_ref[...], two_ref[...], jnp.zeros((14, width), f32)], 0)
        small = small.astype(bf16)
        for n in range(pieces):
            out_ref, k = out_refs[n * 2 // pieces], n % (pieces // 2)
            s = pl.multiple_of(places_ref[n] * feats, 16) if in_place else n * feats
            for p in range(3):
                out_ref[k, p * feats : (p + 1) * feats] = gin_ref[p, pl.ds(s, feats)]
            for f in range(lanes):
                at = pl.ds(f * pieces * feats + s, feats)
                out_ref[k, 3 * feats : 4 * feats, f * mine : (f + 1) * mine] = gout_ref[at]
            out_ref[k, 4 * feats :] = small
            out_ref[k, 4 * feats + 2 : 4 * feats + 5, :mine] = dt_ref[...].astype(bf16)


def add_cores(*refs):
    own_ref, came_ref, out_refs = refs[0], refs[1], refs[2:]
    for r, out_ref in enumerate(out_refs):
        out_ref[...] = (own_ref[r].astype(f32) + came_ref[r].astype(f32)).astype(bf16)


def on_device(tokens, gain_one, gain_two, conv_taps, w_in, w_out, w_gate, w_up, w_down, cotangent):
    seqs, group, width = tokens.shape
    rows = seqs * group
    lanes, line = lax.axis_size("fsdp"), lax.axis_size("line")
    pieces = 2 * line
    count = lanes * pieces
    feats = width // count
    mine = width // lanes
    hid = w_gate.shape[1]
    units = -(-hid // 16) * 16
    blocks = lanes * 2
    f_index = lax.axis_index("fsdp")
    s_index = lax.axis_index(("line", "core"))
    index = lax.axis_index(every)
    onward = [(i, i + 1) for i in range(pieces - 1)]
    back = [(i + 1, i) for i in range(pieces - 1)]

    in_blocks = w_in.T.reshape(3, feats, width)
    routes = [[(k, (3 * k + j) % count) for k in range(count)] for j in range(3)]
    came = jnp.stack([lax.ppermute(in_blocks[j], every, routes[j]) for j in range(3)])
    in_parts = [
        lax.dynamic_index_in_dim(came, (index + p * count) % 3, 0, keepdims=False) for p in range(3)
    ]
    smalls = jnp.pad(jnp.concatenate([gain_one[None], gain_two[None], conv_taps], 0), ((0, 11), (0, 0)))
    smalls = lax.dynamic_update_slice(jnp.zeros((16, mine), bf16), smalls, (0, s_index * feats))
    out_blocks = w_out.T.reshape(feats, lanes, mine).transpose(1, 0, 2)
    out_blocks = jnp.concatenate([out_blocks, jnp.broadcast_to(smalls, (lanes, 16, mine))], 1)
    out_blocks = jnp.concatenate(exchange(out_blocks, "fsdp"), 1)
    edge = lax.ppermute(tokens[:, group - 2 :], ("line", "core"), onward).reshape(2 * seqs, width)
    edge = jnp.pad(edge, ((0, -2 * seqs % 16), (0, 0)))
    mixer_own = tie(jnp.concatenate(in_parts + [out_blocks], 0), edge)
    mixer_slots = gather(mixer_own, "line")
    token_rows = tokens.reshape(rows, width)
    token_slots = gather(tie(jnp.concatenate([token_rows, edge], 0), mixer_own), "fsdp")

    down_rows = tie(w_down.T.reshape(feats, count, hid).transpose(1, 0, 2), mixer_own)
    down_rows = lax.all_to_all(down_rows, every, 0, 0, tiled=True)

    swapped = tie(jnp.stack(mixer_slots), *token_slots[1:], down_rows)
    swapped = flip(swapped, "core", 1)
    cot_rows = cotangent.reshape(rows, width)
    cot_slots = gather(tie(cot_rows, *mixer_slots[1:]), "line")
    z_index, c_index = lax.axis_index("line"), lax.axis_index("core")
    near = [r ^ z_index for r in range(line)]
    places = [2 * z + c_index for z in near]
    places += [2 * z + 1 - c_index for z in near]
    places = jnp.stack(places + [f_index]).astype(jnp.int32)
    anywhere = pl.BlockSpec(memory_space=pl.ANY)
    in_place = feats % 16 == 0 and mine % 128 == 0
    if in_place:
        weights = [places] + mixer_slots + [swapped]
        weight_specs = [pl.BlockSpec(memory_space=pltpu.SMEM)] + [anywhere] * (line + 1)
        weight_outs = [((3, mine, width), bf16, whole((3, mine, width)))]
        weight_outs += [((width, mine), bf16, whole((width, mine)))]
        weight_scratch = [
            pltpu.VMEM((pieces, 16, width), bf16),
            pltpu.SemaphoreType.DMA((pieces * (4 + lanes),)),
        ]
    else:
        mixer_w = jnp.concatenate([jnp.stack(mixer_slots), swapped], 0)[jnp.argsort(places[:-1])]
        full_in = mixer_w[:, : 3 * feats].reshape(pieces, 3, feats, width)
        full_in = full_in.transpose(1, 0, 2, 3).reshape(3, mine, width)
        full_out = mixer_w[:, 3 * feats : 4 * feats].reshape(pieces, feats, lanes, mine)
        full_out = full_out.transpose(2, 0, 1, 3).reshape(width, mine)
        small = jnp.sum(mixer_w[:, 4 * feats :].astype(f32), axis=0)
        taps = lax.dynamic_slice_in_dim(small[2:5], f_index * mine, mine, 1)
        weights = [small, taps, full_in, full_out]
        weight_specs = [whole((16, width)), whole((3, mine))]
        weight_specs += [whole((3, mine, width)), whole((width, mine))]
        weight_outs = weight_scratch = []

    pad = ((0, units - hid), (0, 0))
    gate_up = jnp.concatenate([jnp.pad(w, pad) for w in (w_gate.T, w_up.T)], 0)
    gate_up = lax.all_gather(gate_up, ("fsdp", "core"), axis=0)

    more = token_slots[0].shape[0]
    everyone = lanes * rows
    slot = lambda *shape: pl.BlockSpec((1,) + shape, lambda r: (r,) + (0,) * len(shape))
    per_slot = lambda dtype, *shape: ((lanes,) + shape, dtype, slot(*shape))
    flat = lambda n, count: [((n, width), bf16, whole((n, width)))] * count
    made = kernel_call(
        functools.partial(mixer_forward, seqs, group, lanes, line, in_place),
        (lanes,),
        [whole((more, width))] * lanes + weight_specs,
        flat(rows, lanes)
        + [per_slot(bf16, rows, width)]
        + [per_slot(f32, rows, mine)] * 4
        + [per_slot(bf16, rows, mine), per_slot(bf16, more - rows, mine), per_slot(bf16, rows, mine)]
        + [((16, width), f32, whole((16, width)))]
        + weight_outs,
        [pltpu.VMEM((more, width), bf16)] + weight_scratch,
        24 * everyone * width * mine,
        *token_slots,
        *weights,
    )
    branch_o, held = list(made[:lanes]), made[lanes + 9 :]
    normed_a, b_part, c_part, x_part, conv, gated, halo, branch_y, small = made[lanes : lanes + 9]
    full_in, full_out = held if in_place else weights[2:]
    taps = lax.dynamic_slice_in_dim(small[2:5], f_index * mine, mine, 1)
    branch_o[1] = tie(branch_o[1], cot_slots[-1])
    branch_terms = scatter(branch_o, "fsdp")
    branch_o = total(branch_terms)
    hidden_in = token_rows.astype(f32)
    second = hidden_in + branch_o
    scale_two = lax.rsqrt(jnp.mean(second * second, axis=-1, keepdims=True) + epsilon)
    unit_two = second * scale_two
    normed_u = (unit_two * small[1]).astype(bf16)

    down_rows = down_rows.reshape(width, hid).T
    full_down = tie(jnp.pad(down_rows, pad), gate_up, swapped)
    full_down = lax.all_gather(full_down, ("fsdp", "core"), axis=0)

    some, half_rows = blocks // 2, line // 2 * rows
    third = lambda k: pl.BlockSpec((some, units, width), lambda j: (j, k, 0))
    half = (2, half_rows, some * units)
    per_half = pl.BlockSpec((1,) + half[1:], lambda j: (j, 0, 0))
    slot_specs = [whole((rows, width))] * line
    unit_flops = 2 * line * rows * blocks * units * width
    dhidden = [
        kernel_call(
            functools.partial(hidden_gradient, line // 2),
            (2,),
            slot_specs[: line // 2] + [third(0)],
            [(half, f32, per_half)],
            [],
            unit_flops // 2,
            *cot_slots[odd::2],
            full_down,
        )[0]
        for odd in range(2)
    ]
    normed_u = tie(normed_u, *cot_slots[2::2])
    u_slots = [normed_u] + [None] * (line - 1)
    for r in range(1, line, 2):
        u_slots[r] = flip(normed_u, "line", r)
    held_back = tie(normed_u, *u_slots[1::2], dhidden[1])
    for r in range(2, line, 2):
        u_slots[r] = flip(held_back, "line", r)
    done, du_terms = [None, None], [None] * line
    for odd in (1, 0):
        made = kernel_call(
            functools.partial(feed_forward, line // 2, 2 - odd),
            (2,),
            slot_specs[: line // 2] + [third(0), third(1), per_half],
            [(half, bf16, per_half)] * 3
            + (flat(rows, 1) if odd else flat(rows // 8, 1) + flat(rows - rows // 8, 1)) * (line // 2),
            [pltpu.VMEM((half_rows, width), f32)],
            2 * unit_flops,
            *u_slots[odd::2],
            gate_up,
            gate_up,
            dhidden[odd],
            waits=[] if odd else [done[1][0]],
        )
        done[odd] = made[:3]
        if odd:
            du_terms[1::2] = [flip(d, "line", 2 * n + 1) for n, d in enumerate(made[3:])]
            continue
        du_own, du_parts = jnp.concatenate(made[3:5], 0), []
        for r in range(2, line, 2):
            du_parts += [flip(d, "line", r) for d in made[3 + r : 5 + r]]
            du_terms[r] = jnp.concatenate(du_parts[-2:], 0)
    du_terms[0] = du_own
    ff_grads = lambda kinds, *args: kernel_call(
        functools.partial(feed_forward_grads, line, kinds),
        (2,),
        slot_specs + [per_half] * (2 * kinds),
        [
            (
                (blocks, kinds * units, width),
                bf16,
                pl.BlockSpec((some, kinds * units, width), lambda j: (j, 0, 0)),
            )
        ],
        [pltpu.VMEM((2, half_rows, width), bf16)],
        kinds * unit_flops,
        *args,
    )[0]
    g_ff = ff_grads(2, *u_slots, *done[0][1:], *done[1][1:])
    g_down = ff_grads(1, *cot_slots, done[0][0], done[1][0])
    part_out = kernel_call(
        functools.partial(feed_forward_out, line),
        (2,),
        [per_half, per_half, third(0)],
        flat(rows, line),
        [pltpu.VMEM((line * rows, width), f32)],
        unit_flops,
        done[0][0],
        done[1][0],
        full_down,
    )
    g_down = lax.psum_scatter(tie(g_down, *du_terms[1::2], *du_parts[:1]), ("fsdp", "core"), scatter_dimension=0)
    dunit = total([tie(du_terms[0], part_out[0])] + du_terms[1:])
    out_terms = [tie(p, *du_terms[1::2], *du_parts) for p in part_out[1:]]
    out_terms = scatter([part_out[0]] + out_terms, "line")

    grad_two = jnp.sum(dunit * unit_two, axis=0)
    dnorm_two = dunit * small[1]
    dsecond = cot_rows.astype(f32) + scale_two * (
        dnorm_two - unit_two * jnp.mean(dnorm_two * unit_two, axis=-1, keepdims=True)
    )
    dbranch = dsecond.astype(bf16)
    branch_slots = gather(dbranch, "fsdp")
    everyone = lanes * rows
    dconv, dc_part = kernel_call(
        functools.partial(mixer_backward_one, lanes),
        (lanes,),
        [whole((rows, width))] * lanes + [whole((width, mine)), slot(rows, mine), slot(rows, mine)],
        [per_slot(f32, rows, mine), per_slot(bf16, rows, mine)],
        [pltpu.VMEM((rows, width), bf16)],
        2 * everyone * width * mine,
        *branch_slots,
        full_out,
        c_part,
        conv,
        waits=out_terms[1:-1] + [g_ff],
    )
    block_out = second + total([tie(out_terms[0], dconv)] + out_terms[1:])
    block_out = block_out.astype(bf16).reshape(seqs, group, width)
    g_ff = lax.psum_scatter(tie(g_ff, dconv), ("fsdp", "core"), scatter_dimension=0)
    g_down = g_down[:hid].T.reshape(count, feats, hid)
    ahead = dconv.reshape(lanes, seqs, group, mine)[:, :, :2]
    ahead = lax.ppermute(ahead, ("line", "core"), back).reshape(lanes, 2 * seqs, mine)
    g_rows = 4 * feats + 16
    *dnormed, g_own, g_other = kernel_call(
        functools.partial(mixer_backward_two, seqs, group, pieces, lanes, in_place),
        (lanes,),
        [whole((more, width))] * lanes
        + [whole((rows, width))] * lanes
        + [
            slot(rows, mine),
            slot(2 * seqs, mine),
            slot(rows, mine),
            slot(rows, mine),
            slot(rows, mine),
            slot(rows, mine),
            slot(more - rows, mine),
            whole((3, mine)),
            whole((1, width)),
            whole((3, mine, width)),
            whole((lanes, rows, width)),
            whole((lanes, rows, mine)),
            pl.BlockSpec(memory_space=pltpu.SMEM),
        ],
        flat(rows, lanes)
        + [((line, g_rows, width), bf16, whole((line, g_rows, width)))] * 2,
        [
            pltpu.VMEM((3, lanes, rows, mine), bf16),
            pltpu.VMEM((1, width), f32),
            pltpu.VMEM((3, mine), f32),
            pltpu.VMEM((more, width), bf16),
            pltpu.VMEM((3, mine, width), bf16),
            pltpu.VMEM((width, mine), bf16),
        ],
        14 * everyone * width * mine,
        *token_slots,
        *branch_slots,
        dconv,
        ahead,
        dc_part,
        b_part,
        x_part,
        gated,
        halo,
        taps,
        grad_two[None],
        full_in,
        normed_a,
        branch_y,
        places,
        waits=[g_down],
    )
    if not in_place:
        g_mixer = jnp.concatenate([g_own, g_other], 0)[places[:-1]]
        g_own, g_other = g_mixer[:line], g_mixer[line:]
    g_terms = kernel_call(
        add_cores,
        (1,),
        [whole((line, g_rows, width))] * 2,
        flat(g_rows, line),
        [],
        1,
        g_own,
        flip(tie(g_other, out_terms[-1]), "core", 1),
    )
    g_down = lax.all_to_all(tie(g_down, g_terms[0]), every, 0, 0, tiled=True)
    dnormed = [dnormed[0]] + [tie(d, g_terms[0]) for d in dnormed[1:]]
    g_terms = scatter(g_terms, "line")
    da_terms = [flip(dnormed[r], "fsdp", r) for r in reversed(range(1, lanes))][::-1]
    da_terms = [dnormed[0]] + da_terms
    dnormed = total(da_terms)
    scale_one = lax.rsqrt(jnp.mean(hidden_in * hidden_in, axis=-1, keepdims=True) + epsilon)
    unit_one = hidden_in * scale_one
    dnorm_one = dnormed * small[0]
    dinput = dsecond + scale_one * (
        dnorm_one - unit_one * jnp.mean(dnorm_one * unit_one, axis=-1, keepdims=True)
    )
    grad_tokens = dinput.astype(bf16).reshape(seqs, group, width)

    g_mixer = total(g_terms).astype(bf16)
    g_in = g_mixer[: 3 * feats].reshape(3, feats, width)
    homes = [[(d, k) for k, d in route] for route in routes]
    parts = []
    for j in range(3):
        p = ((j - index) * pow(count, -1, 3)) % 3
        block = lax.dynamic_index_in_dim(g_in, p, 0, keepdims=False)
        parts.append(lax.ppermute(block, every, homes[j]))
    grad_in = jnp.concatenate(parts, 0).T.astype(f32)
    g_out = g_mixer[3 * feats : 4 * feats].reshape(feats, lanes, mine).transpose(1, 0, 2)
    gains = g_mixer[4 * feats : 4 * feats + 2].reshape(2, lanes, pieces, feats)
    gains = lax.dynamic_index_in_dim(gains, s_index, 2, keepdims=False).transpose(1, 0, 2)
    gains = jnp.pad(gains, ((0, 0), (0, 14), (0, mine - feats)))
    got = jnp.stack(exchange(jnp.concatenate([g_out, gains], 1), "fsdp"))
    grad_out = got[:, :feats].transpose(0, 2, 1).reshape(width, feats).astype(f32)
    gains = jnp.sum(got[:, feats : feats + 2, :feats].astype(f32), axis=0)
    grad_taps = g_mixer[4 * feats + 2 : 4 * feats + 5, :mine].reshape(3, pieces, feats)
    grad_taps = lax.dynamic_index_in_dim(grad_taps, s_index, 1, keepdims=False).astype(f32)
    grad_gate = g_ff[:hid].T.astype(f32)
    grad_up = g_ff[units : units + hid].T.astype(f32)
    grad_down = g_down.transpose(0, 2, 1).reshape(count * hid, feats).astype(f32)
    return (
        block_out,
        grad_tokens,
        gains[0],
        gains[1],
        grad_taps,
        grad_in,
        grad_out,
        grad_gate,
        grad_up,
        grad_down,
    )


def solution(mesh):
    lanes, pieces = mesh.devices.shape
    fine = Mesh(mesh.devices.reshape(lanes, pieces // 2, 2), every)
    token = P("fsdp", ("line", "core"), None)
    vector = P(every)
    columns = P(None, every)
    return jax.shard_map(
        on_device,
        mesh=fine,
        in_specs=(token, vector, vector) + (columns,) * 6 + (token,),
        out_specs=(token, token, vector, vector) + (columns,) * 6,
        check_vma=False,
    )
```

```python
import functools

import jax
import jax.numpy as jnp
from jax import lax
from jax.experimental import pallas as pl
from jax.experimental.pallas import tpu as pltpu
from jax.sharding import Mesh, PartitionSpec as P

epsilon = 1e-05
every = ("fsdp", "line", "core")
bf16 = jnp.bfloat16
f32 = jnp.float32
vmem_bytes = 58 * 2**20


def dot(left, right):
    return jnp.dot(left, right, preferred_element_type=f32)


def dot_nt(left, right):
    return lax.dot_general(left, right, (((1,), (1,)), ((), ())), preferred_element_type=f32)


def dot_tn(left, right):
    return lax.dot_general(left, right, (((0,), (0,)), ((), ())), preferred_element_type=f32)


def tie(block, *earlier):
    anywhere = pl.BlockSpec(memory_space=pl.ANY)
    return pl.pallas_call(
        lambda *refs: None,
        in_specs=[anywhere] * (1 + len(earlier)),
        out_specs=anywhere,
        out_shape=jax.ShapeDtypeStruct(block.shape, block.dtype),
        input_output_aliases={0: 0},
    )(block, *earlier)


def flip(block, axis, bits):
    size = lax.axis_size(axis)
    return lax.ppermute(block, axis, [(i, i ^ bits) for i in range(size)])


def gather(block, axis):
    return [block] + [flip(block, axis, r) for r in range(1, lax.axis_size(axis))]


def scatter(slots, axis):
    return [slots[0]] + [flip(slots[r], axis, r) for r in range(1, lax.axis_size(axis))]


def total(terms):
    return sum(t.astype(f32) for t in terms)


def exchange(blocks, axis):
    size = lax.axis_size(axis)
    me = lax.axis_index(axis)
    came = []
    for r in range(size):
        sent = lax.dynamic_index_in_dim(blocks, me ^ r, 0, keepdims=False)
        came.append(flip(sent, axis, r) if r else sent)
    out = []
    for d in range(size):
        block = came[0]
        for r in range(1, size):
            block = jnp.where(me ^ r == d, came[r], block)
        out.append(block)
    return out


def whole(shape):
    return pl.BlockSpec(shape, lambda *_: (0,) * len(shape))


def kernel_call(body, grid, ins, outs, scratch, flops, *args, waits=()):
    held = len(args)
    shapes = [jax.ShapeDtypeStruct(shape, dtype) for shape, dtype, _ in outs]
    moved = sum(a.size * a.dtype.itemsize for a in args)
    moved = (moved + sum(s.size * s.dtype.itemsize for s in shapes)) * (flops > 0)
    return pl.pallas_call(
        lambda *refs: body(*refs[:held], *refs[held + len(waits) :]),
        grid=grid,
        in_specs=ins + [pl.BlockSpec(memory_space=pl.ANY)] * len(waits),
        out_specs=[spec for _, _, spec in outs],
        out_shape=shapes,
        scratch_shapes=scratch,
        compiler_params=pltpu.CompilerParams(
            dimension_semantics=("arbitrary",) * len(grid), vmem_limit_bytes=vmem_bytes
        ),
        cost_estimate=pl.CostEstimate(flops=flops, bytes_accessed=moved, transcendentals=0),
    )(*args, *waits)


def shifted(block, distance, edge):
    rows = block.shape[0]
    moved = pltpu.roll(block, distance % rows, 0)
    row = lax.broadcasted_iota(jnp.int32, block.shape, 0)
    for n in range(abs(distance)):
        at = n if distance > 0 else rows - abs(distance) + n
        moved = jnp.where(row == at, edge[n : n + 1], moved)
    return moved


def mixer_forward(seqs, group, lanes, line, in_place, *refs):
    tok_refs, refs = refs[:lanes], refs[lanes:]
    if in_place:
        places_ref, source_refs, other, refs = refs[0], refs[1 : 1 + line], refs[1 + line], refs[2 + line :]
        source_refs = list(source_refs) + [other.at[r] for r in range(line)]
        win_ref, wout_ref = refs[lanes + 9 : lanes + 11]
        bring_weights(2 * line, places_ref, source_refs, win_ref, wout_ref, *refs[-2:])
    else:
        (added_ref, taps_ref, win_ref, wout_ref), refs = refs[:4], refs[4:]
    part_refs, refs = refs[:lanes], refs[lanes:]
    norm_ref, b_ref, c_ref, x_ref, conv_ref, gated_ref, halo_ref, y_ref, small_ref = refs[:9]
    tok_ref = refs[11 if in_place else 9]

    @pl.when(pl.program_id(0) == 0)
    def _():
        if in_place:
            small_ref[...] = sum(refs[-2][k].astype(f32) for k in range(2 * line))
        else:
            small_ref[...] = added_ref[...]

    gain_ref = small_ref.at[0:1]
    if in_place:
        mine = wout_ref.shape[1]
        at = pl.multiple_of(places_ref[2 * line] * mine, 128)
        taps_ref = small_ref.at[2:5, pl.ds(at, mine)]
    pick(tok_refs, tok_ref)
    rows = seqs * group
    h = tok_ref[...].astype(f32)
    unit = h * lax.rsqrt(jnp.mean(h * h, axis=-1, keepdims=True) + epsilon)
    norm = (unit * gain_ref[...]).astype(bf16)
    norm_ref[0] = norm[:rows]
    b_all, x_all = dot_nt(norm, win_ref[0]), dot_nt(norm, win_ref[2])
    c_part = dot_nt(norm[:rows], win_ref[1])
    b_ref[0], c_ref[0], x_ref[0] = b_all[:rows], c_part, x_all[:rows]
    gated = (b_all * x_all).astype(bf16)
    gated_ref[0], halo_ref[0] = gated[:rows], gated[rows:]
    halo = gated[rows:].astype(f32)
    for q in range(seqs):
        at = slice(q * group, (q + 1) * group)
        now = gated[at].astype(f32)
        edge = halo[2 * q : 2 * q + 2]
        conv = (
            taps_ref[0:1] * shifted(now, 2, edge)
            + taps_ref[1:2] * shifted(now, 1, edge[1:])
            + taps_ref[2:3] * now
        )
        conv_ref[0, at] = conv
        y_ref[0, at] = (c_part[at] * conv).astype(bf16)
    hand(dot_nt(y_ref[0], wout_ref[...]).astype(bf16), part_refs)


def merged(ref):
    n, units, width = ref.shape
    return ref[...].reshape(n * units, width)


def hidden_gradient(n, *refs):
    cot_refs, down_ref, out_ref = refs[:n], refs[n], refs[n + 1]
    w_down = merged(down_ref)
    rows = cot_refs[0].shape[0]
    for r in range(n):
        out_ref[0, r * rows : (r + 1) * rows] = dot_nt(cot_refs[r][...], w_down)


def add_up(acc_ref, at, part, out_ref):
    j = pl.program_id(0)

    @pl.when(j == 0)
    def _():
        acc_ref[at] = part

    @pl.when(j == 1)
    def _():
        out_ref[...] = (acc_ref[at] + part).astype(bf16)


def feed_forward(n, parts, *refs):
    u_refs, (gate_ref, up_ref, dh_ref), refs = refs[:n], refs[n : n + 3], refs[n + 3 :]
    (hid_ref, dg_ref, dup_ref), du_refs, acc_ref = refs[:3], refs[3:-1], refs[-1]
    w_gate, w_up = merged(gate_ref), merged(up_ref)
    rows = u_refs[0].shape[0]
    for r in range(n):
        at = slice(r * rows, (r + 1) * rows)
        gate = dot_nt(u_refs[r][...], w_gate)
        up = dot_nt(u_refs[r][...], w_up)
        dh = dh_ref[0, at]
        sig = jax.nn.sigmoid(gate)
        silu = gate * sig
        hid_ref[0, at] = (silu * up).astype(bf16)
        dgate = (dh * up * sig * (1.0 + gate * (1.0 - sig))).astype(bf16)
        dup = (dh * silu).astype(bf16)
        dg_ref[0, at] = dgate
        dup_ref[0, at] = dup
        du = dot(dgate, w_gate) + dot(dup, w_up)
        ends = [0, rows // 8, rows] if parts == 2 else [0, rows]
        for h in range(parts):
            here = slice(r * rows + ends[h], r * rows + ends[h + 1])
            add_up(acc_ref, here, du[ends[h] : ends[h + 1]], du_refs[r * parts + h])


def feed_forward_out(line, *refs):
    hid_refs, down_ref, out_refs, acc_ref = refs[:2], refs[2], refs[3 : 3 + line], refs[3 + line]
    w_down = merged(down_ref)
    rows = out_refs[0].shape[0]
    for r in range(line):
        part = dot(hid_refs[r % 2][0, r // 2 * rows : (r // 2 + 1) * rows], w_down)
        add_up(acc_ref, slice(r * rows, (r + 1) * rows), part, out_refs[r])


def feed_forward_grads(line, kinds, *refs):
    right_refs, halves, refs = refs[:line], refs[line : line + 2 * kinds], refs[line + 2 * kinds :]
    out_ref, right_all = refs
    rows = right_refs[0].shape[0]

    @pl.when(pl.program_id(0) == 0)
    def _():
        for r in range(line):
            right_all[r % 2, r // 2 * rows : (r // 2 + 1) * rows] = right_refs[r][...]

    n, units, width = out_ref.shape
    units //= kinds
    for k in range(kinds):
        part = sum(dot_tn(halves[h * kinds + k][0], right_all[h]) for h in range(2))
        out_ref[:, k * units : (k + 1) * units] = part.astype(bf16).reshape(n, units, width)


def pick(slot_refs, out_ref):
    for r, ref in enumerate(slot_refs):

        @pl.when(pl.program_id(0) == r)
        def _(ref=ref):
            out_ref[...] = ref[...]


def hand(block, out_refs):
    for r, ref in enumerate(out_refs):

        @pl.when(pl.program_id(0) == r)
        def _(ref=ref):
            ref[...] = block


def bring_weights(pieces, places_ref, sources, win_ref, wout_ref, small_ref, sems):
    width, mine = wout_ref.shape
    feats = mine // pieces
    copies = []
    for k, source in enumerate(sources):
        s = places_ref[k]
        for p in range(3):
            rows = pl.ds(pl.multiple_of(s * feats, 16), feats)
            copies.append((source.at[pl.ds(p * feats, feats)], win_ref.at[p, rows]))
        for f in range(width // mine):
            rows = pl.ds(pl.multiple_of((f * pieces + s) * feats, 16), feats)
            columns = source.at[pl.ds(3 * feats, feats), pl.ds(f * mine, mine)]
            copies.append((columns, wout_ref.at[rows]))
        copies.append((source.at[pl.ds(4 * feats, 16)], small_ref.at[k]))
    copies = [pltpu.make_async_copy(a, b, sems.at[n]) for n, (a, b) in enumerate(copies)]

    @pl.when(pl.program_id(0) == 0)
    def _():
        for copy in copies:
            copy.start()
        for copy in copies:
            copy.wait()


def mixer_backward_one(lanes, *refs):
    branch_refs, (wout_ref, c_ref, conv_ref, dconv_ref, dc_ref, now_ref) = refs[:lanes], refs[lanes:]
    pick(branch_refs, now_ref)
    dy = dot(now_ref[...], wout_ref[...])
    dconv_ref[0] = dy * c_ref[0]
    dc_ref[0] = (dy * conv_ref[0]).astype(bf16)


def mixer_backward_two(seqs, group, pieces, lanes, in_place, *refs):
    tok_refs, branch_refs, refs = refs[:lanes], refs[lanes : 2 * lanes], refs[2 * lanes :]
    (dconv_ref, ahead_ref, dc_ref, b_ref, x_ref, gated_ref, halo_ref, taps_ref, two_ref) = refs[:9]
    (win_ref, norm_ref, y_ref, places_ref), refs = refs[9:13], refs[13:]
    part_refs, out_refs, refs = refs[:lanes], refs[lanes : lanes + 2], refs[lanes + 2 :]
    dm_ref, one_ref, dt_ref, tok_ref, gin_ref, gout_ref = refs
    pick(tok_refs, tok_ref)
    r = pl.program_id(0)
    rows = seqs * group
    width = norm_ref.shape[2]
    mine = win_ref.shape[1]

    @pl.when(r == 0)
    def _():
        one_ref[...] = jnp.zeros_like(one_ref)
        dt_ref[...] = jnp.zeros_like(dt_ref)

    for q in range(seqs):
        at = slice(q * group, (q + 1) * group)
        now = dconv_ref[0, at]
        edge = ahead_ref[0, 2 * q : 2 * q + 2]
        dgated = (
            taps_ref[2:3] * now
            + taps_ref[1:2] * shifted(now, -1, edge)
            + taps_ref[0:1] * shifted(now, -2, edge)
        )
        dm_ref[0, r, at] = (dgated * x_ref[0, at]).astype(bf16)
        dm_ref[2, r, at] = (dgated * b_ref[0, at]).astype(bf16)
        held = gated_ref[0, at].astype(f32)
        past = halo_ref[0].astype(f32)[2 * q : 2 * q + 2]
        for k, block in enumerate((shifted(held, 2, past), shifted(held, 1, past[1:]), held)):
            dt_ref[k : k + 1] += jnp.sum(now * block, axis=0, keepdims=True)
    dm_ref[1, r] = dc_ref[0]
    da = sum(dot(dm_ref[p, r], win_ref[p]) for p in range(3))
    hand(da.astype(bf16), part_refs)
    h = tok_ref[:rows].astype(f32)
    unit = h * lax.rsqrt(jnp.mean(h * h, axis=-1, keepdims=True) + epsilon)
    one_ref[...] += jnp.sum(da * unit, axis=0, keepdims=True)

    @pl.when(r == pl.num_programs(0) - 1)
    def _():
        slots = norm_ref.shape[0]
        feats = mine // pieces
        norm = norm_ref[...].reshape(slots * rows, width)
        for p in range(3):
            gin_ref[p] = dot_tn(dm_ref[p].reshape(slots * rows, mine), norm).astype(bf16)
        g_out = sum(dot_tn(branch_refs[f][...], y_ref[f]) for f in range(lanes))
        gout_ref[...] = g_out.astype(bf16)
        small = jnp.concatenate([one_ref[...], two_ref[...], jnp.zeros((14, width), f32)], 0)
        small = small.astype(bf16)
        for n in range(pieces):
            out_ref, k = out_refs[n * 2 // pieces], n % (pieces // 2)
            s = pl.multiple_of(places_ref[n] * feats, 16) if in_place else n * feats
            for p in range(3):
                out_ref[k, p * feats : (p + 1) * feats] = gin_ref[p, pl.ds(s, feats)]
            for f in range(lanes):
                at = pl.ds(f * pieces * feats + s, feats)
                out_ref[k, 3 * feats : 4 * feats, f * mine : (f + 1) * mine] = gout_ref[at]
            out_ref[k, 4 * feats :] = small
            out_ref[k, 4 * feats + 2 : 4 * feats + 5, :mine] = dt_ref[...].astype(bf16)


def add_cores(*refs):
    own_ref, came_ref, out_refs = refs[0], refs[1], refs[2:]
    for r, out_ref in enumerate(out_refs):
        out_ref[...] = (own_ref[r].astype(f32) + came_ref[r].astype(f32)).astype(bf16)


def on_device(tokens, gain_one, gain_two, conv_taps, w_in, w_out, w_gate, w_up, w_down, cotangent):
    seqs, group, width = tokens.shape
    rows = seqs * group
    lanes, line = lax.axis_size("fsdp"), lax.axis_size("line")
    pieces = 2 * line
    count = lanes * pieces
    feats = width // count
    mine = width // lanes
    hid = w_gate.shape[1]
    units = -(-hid // 16) * 16
    blocks = lanes * 2
    f_index = lax.axis_index("fsdp")
    s_index = lax.axis_index(("line", "core"))
    index = lax.axis_index(every)
    onward = [(i, i + 1) for i in range(pieces - 1)]
    back = [(i + 1, i) for i in range(pieces - 1)]

    in_blocks = w_in.T.reshape(3, feats, width)
    routes = [[(k, (3 * k + j) % count) for k in range(count)] for j in range(3)]
    came = jnp.stack([lax.ppermute(in_blocks[j], every, routes[j]) for j in range(3)])
    in_parts = [
        lax.dynamic_index_in_dim(came, (index + p * count) % 3, 0, keepdims=False) for p in range(3)
    ]
    smalls = jnp.pad(jnp.concatenate([gain_one[None], gain_two[None], conv_taps], 0), ((0, 11), (0, 0)))
    smalls = lax.dynamic_update_slice(jnp.zeros((16, mine), bf16), smalls, (0, s_index * feats))
    out_blocks = w_out.T.reshape(feats, lanes, mine).transpose(1, 0, 2)
    out_blocks = jnp.concatenate([out_blocks, jnp.broadcast_to(smalls, (lanes, 16, mine))], 1)
    out_blocks = jnp.concatenate(exchange(out_blocks, "fsdp"), 1)
    edge = lax.ppermute(tokens[:, group - 2 :], ("line", "core"), onward).reshape(2 * seqs, width)
    edge = jnp.pad(edge, ((0, -2 * seqs % 16), (0, 0)))
    mixer_own = tie(jnp.concatenate(in_parts + [out_blocks], 0), edge)
    mixer_slots = gather(mixer_own, "line")
    token_rows = tokens.reshape(rows, width)
    token_slots = gather(tie(jnp.concatenate([token_rows, edge], 0), mixer_own), "fsdp")

    down_rows = tie(w_down.T.reshape(feats, count, hid).transpose(1, 0, 2), mixer_own)
    down_rows = lax.all_to_all(down_rows, every, 0, 0, tiled=True)

    swapped = tie(jnp.stack(mixer_slots), *token_slots[1:], down_rows)
    swapped = flip(swapped, "core", 1)
    cot_rows = cotangent.reshape(rows, width)
    cot_slots = gather(tie(cot_rows, *mixer_slots[1:]), "line")
    z_index, c_index = lax.axis_index("line"), lax.axis_index("core")
    near = [r ^ z_index for r in range(line)]
    places = [2 * z + c_index for z in near]
    places += [2 * z + 1 - c_index for z in near]
    places = jnp.stack(places + [f_index]).astype(jnp.int32)
    anywhere = pl.BlockSpec(memory_space=pl.ANY)
    in_place = feats % 16 == 0 and mine % 128 == 0
    if in_place:
        weights = [places] + mixer_slots + [swapped]
        weight_specs = [pl.BlockSpec(memory_space=pltpu.SMEM)] + [anywhere] * (line + 1)
        weight_outs = [((3, mine, width), bf16, whole((3, mine, width)))]
        weight_outs += [((width, mine), bf16, whole((width, mine)))]
        weight_scratch = [
            pltpu.VMEM((pieces, 16, width), bf16),
            pltpu.SemaphoreType.DMA((pieces * (4 + lanes),)),
        ]
    else:
        mixer_w = jnp.concatenate([jnp.stack(mixer_slots), swapped], 0)[jnp.argsort(places[:-1])]
        full_in = mixer_w[:, : 3 * feats].reshape(pieces, 3, feats, width)
        full_in = full_in.transpose(1, 0, 2, 3).reshape(3, mine, width)
        full_out = mixer_w[:, 3 * feats : 4 * feats].reshape(pieces, feats, lanes, mine)
        full_out = full_out.transpose(2, 0, 1, 3).reshape(width, mine)
        small = jnp.sum(mixer_w[:, 4 * feats :].astype(f32), axis=0)
        taps = lax.dynamic_slice_in_dim(small[2:5], f_index * mine, mine, 1)
        weights = [small, taps, full_in, full_out]
        weight_specs = [whole((16, width)), whole((3, mine))]
        weight_specs += [whole((3, mine, width)), whole((width, mine))]
        weight_outs = weight_scratch = []

    pad = ((0, units - hid), (0, 0))
    gate_up = jnp.concatenate([jnp.pad(w, pad) for w in (w_gate.T, w_up.T)], 0)
    gate_up = lax.all_gather(gate_up, ("fsdp", "core"), axis=0)

    more = token_slots[0].shape[0]
    everyone = lanes * rows
    slot = lambda *shape: pl.BlockSpec((1,) + shape, lambda r: (r,) + (0,) * len(shape))
    per_slot = lambda dtype, *shape: ((lanes,) + shape, dtype, slot(*shape))
    flat = lambda n, count: [((n, width), bf16, whole((n, width)))] * count
    made = kernel_call(
        functools.partial(mixer_forward, seqs, group, lanes, line, in_place),
        (lanes,),
        [whole((more, width))] * lanes + weight_specs,
        flat(rows, lanes)
        + [per_slot(bf16, rows, width)]
        + [per_slot(f32, rows, mine)] * 4
        + [per_slot(bf16, rows, mine), per_slot(bf16, more - rows, mine), per_slot(bf16, rows, mine)]
        + [((16, width), f32, whole((16, width)))]
        + weight_outs,
        [pltpu.VMEM((more, width), bf16)] + weight_scratch,
        24 * everyone * width * mine,
        *token_slots,
        *weights,
    )
    branch_o, held = list(made[:lanes]), made[lanes + 9 :]
    normed_a, b_part, c_part, x_part, conv, gated, halo, branch_y, small = made[lanes : lanes + 9]
    full_in, full_out = held if in_place else weights[2:]
    taps = lax.dynamic_slice_in_dim(small[2:5], f_index * mine, mine, 1)
    branch_o[1] = tie(branch_o[1], cot_slots[-1])
    branch_terms = scatter(branch_o, "fsdp")
    branch_o = total(branch_terms)
    hidden_in = token_rows.astype(f32)
    second = hidden_in + branch_o
    scale_two = lax.rsqrt(jnp.mean(second * second, axis=-1, keepdims=True) + epsilon)
    unit_two = second * scale_two
    normed_u = (unit_two * small[1]).astype(bf16)

    down_rows = down_rows.reshape(width, hid).T
    full_down = tie(jnp.pad(down_rows, pad), gate_up, swapped)
    full_down = lax.all_gather(full_down, ("fsdp", "core"), axis=0)

    some, half_rows = blocks // 2, line // 2 * rows
    third = lambda k: pl.BlockSpec((some, units, width), lambda j: (j, k, 0))
    half = (2, half_rows, some * units)
    per_half = pl.BlockSpec((1,) + half[1:], lambda j: (j, 0, 0))
    slot_specs = [whole((rows, width))] * line
    unit_flops = 2 * line * rows * blocks * units * width
    dhidden = [
        kernel_call(
            functools.partial(hidden_gradient, line // 2),
            (2,),
            slot_specs[: line // 2] + [third(0)],
            [(half, f32, per_half)],
            [],
            unit_flops // 2,
            *cot_slots[odd::2],
            full_down,
        )[0]
        for odd in range(2)
    ]
    normed_u = tie(normed_u, *cot_slots[2::2])
    u_slots = [normed_u] + [None] * (line - 1)
    for r in range(1, line, 2):
        u_slots[r] = flip(normed_u, "line", r)
    held_back = tie(normed_u, *u_slots[1::2], dhidden[1])
    for r in range(2, line, 2):
        u_slots[r] = flip(held_back, "line", r)
    done, du_terms = [None, None], [None] * line
    for odd in (1, 0):
        made = kernel_call(
            functools.partial(feed_forward, line // 2, 2 - odd),
            (2,),
            slot_specs[: line // 2] + [third(0), third(1), per_half],
            [(half, bf16, per_half)] * 3
            + (flat(rows, 1) if odd else flat(rows // 8, 1) + flat(rows - rows // 8, 1)) * (line // 2),
            [pltpu.VMEM((half_rows, width), f32)],
            2 * unit_flops,
            *u_slots[odd::2],
            gate_up,
            gate_up,
            dhidden[odd],
            waits=[] if odd else [done[1][0]],
        )
        done[odd] = made[:3]
        if odd:
            du_terms[1::2] = [flip(d, "line", 2 * n + 1) for n, d in enumerate(made[3:])]
            continue
        du_own, du_parts = jnp.concatenate(made[3:5], 0), []
        for r in range(2, line, 2):
            du_parts += [flip(d, "line", r) for d in made[3 + r : 5 + r]]
            du_terms[r] = jnp.concatenate(du_parts[-2:], 0)
    du_terms[0] = du_own
    ff_grads = lambda kinds, *args: kernel_call(
        functools.partial(feed_forward_grads, line, kinds),
        (2,),
        slot_specs + [per_half] * (2 * kinds),
        [
            (
                (blocks, kinds * units, width),
                bf16,
                pl.BlockSpec((some, kinds * units, width), lambda j: (j, 0, 0)),
            )
        ],
        [pltpu.VMEM((2, half_rows, width), bf16)],
        kinds * unit_flops,
        *args,
    )[0]
    g_ff = ff_grads(2, *u_slots, *done[0][1:], *done[1][1:])
    g_down = ff_grads(1, *cot_slots, done[0][0], done[1][0])
    part_out = kernel_call(
        functools.partial(feed_forward_out, line),
        (2,),
        [per_half, per_half, third(0)],
        flat(rows, line),
        [pltpu.VMEM((line * rows, width), f32)],
        unit_flops,
        done[0][0],
        done[1][0],
        full_down,
    )
    g_down = lax.psum_scatter(tie(g_down, *du_terms[1::2], *du_parts[:1]), ("fsdp", "core"), scatter_dimension=0)
    dunit = total([tie(du_terms[0], part_out[0])] + du_terms[1:])
    out_terms = [tie(p, *du_terms[1::2], *du_parts) for p in part_out[1:]]
    out_terms = scatter([part_out[0]] + out_terms, "line")

    grad_two = jnp.sum(dunit * unit_two, axis=0)
    dnorm_two = dunit * small[1]
    dsecond = cot_rows.astype(f32) + scale_two * (
        dnorm_two - unit_two * jnp.mean(dnorm_two * unit_two, axis=-1, keepdims=True)
    )
    dbranch = dsecond.astype(bf16)
    branch_slots = gather(dbranch, "fsdp")
    everyone = lanes * rows
    dconv, dc_part = kernel_call(
        functools.partial(mixer_backward_one, lanes),
        (lanes,),
        [whole((rows, width))] * lanes + [whole((width, mine)), slot(rows, mine), slot(rows, mine)],
        [per_slot(f32, rows, mine), per_slot(bf16, rows, mine)],
        [pltpu.VMEM((rows, width), bf16)],
        2 * everyone * width * mine,
        *branch_slots,
        full_out,
        c_part,
        conv,
        waits=out_terms[1:-1] + [g_ff],
    )
    block_out = second + total([tie(out_terms[0], dconv)] + out_terms[1:])
    block_out = block_out.astype(bf16).reshape(seqs, group, width)
    g_ff = lax.psum_scatter(tie(g_ff, *branch_slots[1:]), ("fsdp", "core"), scatter_dimension=0)
    g_down = g_down[:hid].T.reshape(count, feats, hid)
    ahead = dconv.reshape(lanes, seqs, group, mine)[:, :, :2]
    ahead = lax.ppermute(ahead, ("line", "core"), back).reshape(lanes, 2 * seqs, mine)
    g_rows = 4 * feats + 16
    *dnormed, g_own, g_other = kernel_call(
        functools.partial(mixer_backward_two, seqs, group, pieces, lanes, in_place),
        (lanes,),
        [whole((more, width))] * lanes
        + [whole((rows, width))] * lanes
        + [
            slot(rows, mine),
            slot(2 * seqs, mine),
            slot(rows, mine),
            slot(rows, mine),
            slot(rows, mine),
            slot(rows, mine),
            slot(more - rows, mine),
            whole((3, mine)),
            whole((1, width)),
            whole((3, mine, width)),
            whole((lanes, rows, width)),
            whole((lanes, rows, mine)),
            pl.BlockSpec(memory_space=pltpu.SMEM),
        ],
        flat(rows, lanes)
        + [((line, g_rows, width), bf16, whole((line, g_rows, width)))] * 2,
        [
            pltpu.VMEM((3, lanes, rows, mine), bf16),
            pltpu.VMEM((1, width), f32),
            pltpu.VMEM((3, mine), f32),
            pltpu.VMEM((more, width), bf16),
            pltpu.VMEM((3, mine, width), bf16),
            pltpu.VMEM((width, mine), bf16),
        ],
        14 * everyone * width * mine,
        *token_slots,
        *branch_slots,
        dconv,
        ahead,
        dc_part,
        b_part,
        x_part,
        gated,
        halo,
        taps,
        grad_two[None],
        full_in,
        normed_a,
        branch_y,
        places,
        waits=[g_down],
    )
    if not in_place:
        g_mixer = jnp.concatenate([g_own, g_other], 0)[places[:-1]]
        g_own, g_other = g_mixer[:line], g_mixer[line:]
    g_terms = kernel_call(
        add_cores,
        (1,),
        [whole((line, g_rows, width))] * 2,
        flat(g_rows, line),
        [],
        1,
        g_own,
        flip(tie(g_other, out_terms[-1]), "core", 1),
    )
    g_down = lax.all_to_all(tie(g_down, g_terms[0]), every, 0, 0, tiled=True)
    dnormed = [dnormed[0]] + [tie(d, g_terms[0]) for d in dnormed[1:]]
    g_terms = scatter(g_terms, "line")
    da_terms = [flip(dnormed[r], "fsdp", r) for r in reversed(range(1, lanes))][::-1]
    da_terms = [dnormed[0]] + da_terms
    dnormed = total(da_terms)
    scale_one = lax.rsqrt(jnp.mean(hidden_in * hidden_in, axis=-1, keepdims=True) + epsilon)
    unit_one = hidden_in * scale_one
    dnorm_one = dnormed * small[0]
    dinput = dsecond + scale_one * (
        dnorm_one - unit_one * jnp.mean(dnorm_one * unit_one, axis=-1, keepdims=True)
    )
    grad_tokens = dinput.astype(bf16).reshape(seqs, group, width)

    g_mixer = total(g_terms).astype(bf16)
    g_in = g_mixer[: 3 * feats].reshape(3, feats, width)
    homes = [[(d, k) for k, d in route] for route in routes]
    parts = []
    for j in range(3):
        p = ((j - index) * pow(count, -1, 3)) % 3
        block = lax.dynamic_index_in_dim(g_in, p, 0, keepdims=False)
        parts.append(lax.ppermute(block, every, homes[j]))
    grad_in = jnp.concatenate(parts, 0).T.astype(f32)
    g_out = g_mixer[3 * feats : 4 * feats].reshape(feats, lanes, mine).transpose(1, 0, 2)
    gains = g_mixer[4 * feats : 4 * feats + 2].reshape(2, lanes, pieces, feats)
    gains = lax.dynamic_index_in_dim(gains, s_index, 2, keepdims=False).transpose(1, 0, 2)
    gains = jnp.pad(gains, ((0, 0), (0, 14), (0, mine - feats)))
    got = jnp.stack(exchange(jnp.concatenate([g_out, gains], 1), "fsdp"))
    grad_out = got[:, :feats].transpose(0, 2, 1).reshape(width, feats).astype(f32)
    gains = jnp.sum(got[:, feats : feats + 2, :feats].astype(f32), axis=0)
    grad_taps = g_mixer[4 * feats + 2 : 4 * feats + 5, :mine].reshape(3, pieces, feats)
    grad_taps = lax.dynamic_index_in_dim(grad_taps, s_index, 1, keepdims=False).astype(f32)
    grad_gate = g_ff[:hid].T.astype(f32)
    grad_up = g_ff[units : units + hid].T.astype(f32)
    grad_down = g_down.transpose(0, 2, 1).reshape(count * hid, feats).astype(f32)
    return (
        block_out,
        grad_tokens,
        gains[0],
        gains[1],
        grad_taps,
        grad_in,
        grad_out,
        grad_gate,
        grad_up,
        grad_down,
    )


def solution(mesh):
    lanes, pieces = mesh.devices.shape
    fine = Mesh(mesh.devices.reshape(lanes, pieces // 2, 2), every)
    token = P("fsdp", ("line", "core"), None)
    vector = P(every)
    columns = P(None, every)
    return jax.shard_map(
        on_device,
        mesh=fine,
        in_specs=(token, vector, vector) + (columns,) * 6 + (token,),
        out_specs=(token, token, vector, vector) + (columns,) * 6,
        check_vma=False,
    )
```
